32 devices in a mesh: seq: 8 (over z, core), batch: 4 (over y, x).
Axes of the slice: x: 2, y: 2, z: 4, core: 2. Of those that a mesh axis runs over, the one named last changes fastest.
Arguments:
- events: bfloat16 [8, 1024, 1024], P('batch', 'seq'), may hold values from -6 to 6
- w_in: bfloat16 [1024, 4096], P(None, 'batch'), may hold values from -0.1875 to 0.1875
- w_out: bfloat16 [1024, 1024], replicated, may hold values from -0.1875 to 0.1875
- item_table: bfloat16 [4096, 1024], P(('seq', 'batch')), may hold values from -6 to 6
- item_bias: bfloat16 [4096], P(('seq', 'batch')), may hold values from -10 to -6
- segment_lengths: int32 [8, 8], P('batch'), may hold values from 1 to 512, 1024 in all within a row
- listed_pos: int32 [64, 8], P(None, 'batch'), may hold values from 0 to 1023
- labels: int32 [64, 8], P(None, 'batch'), may hold values from 0 to 4095
Outputs:
- layer_out: bfloat16 [8, 1024, 1024], P('batch', 'seq')
- hidden_grad: float32 [64, 8, 1024], P('seq', 'batch')
The draws below stay inside these ranges and needn't reach their ends.
Inputs may be any that keep to these rules, and one draw needn't show every extreme that they name: `segment_lengths`: each row holds 8 lengths that sum to 1024; its largest is exactly 512.
All inputs are finite; a program needn't handle non-finite values.
Results may differ from the reference program's by a relative error of at most 0.0065.
Values may be sent and summed in bfloat16 or wider, within the bound.
No kernel may reach another device: no remote copies, remote signals or barrier semaphores. Data moves between devices by JAX's collectives and lax.ppermute only.
A program may use at most 64 MiB of HBM per device.

```python
import math
import jax
import jax.numpy as jnp
import numpy as np
from jax import lax

HEADS = 16
HD = 64
D = 1024
LEN = 1024
HIST = 8
SEGS = 8
LIST_HIST = 64
IDEV = 128
ITEMS = 4096


def set_ends(drawn, rng, least, largest):
    longest = drawn.shape.index(max(drawn.shape))
    spots = []
    for shift in (0, 1):
        where = [jax.random.randint(jax.random.fold_in(rng, axis), (), 0, length) for axis, length in enumerate(drawn.shape)]
        where[longest] = (where[longest] + shift) % drawn.shape[longest]
        spots.append(tuple(where))
    return drawn.at[spots[0]].set(least).at[spots[1]].set(largest)


def levels(stream_key, dims, cuts, least, top_value):
    def one(dim, parts):
        steps = jax.random.uniform(jax.random.fold_in(jax.random.fold_in(stream_key, 6), dim), (parts,), jnp.float32, least / len(cuts), top_value / len(cuts))
        return jnp.repeat(jnp.exp(steps), dims[dim] // parts).reshape((-1,) + (1,) * (len(dims) - dim - 1))

    level = one(*cuts[0])
    for cut in cuts[1:]:
        level = level * one(*cut)
    return level


def length_profile(count, total, most, slope):
    loads = [(1 << 20) // math.isqrt(rank ** slope) + 1 for rank in range(2, count + 1)]
    surplus, counts = total - most - (count - 1), [1] * (count - 1)
    while surplus > 0:
        free = [i for i in range(count - 1) if counts[i] < most]
        whole, remaining = sum([loads[i] for i in free]), surplus
        for i in free:
            extra = min(most - counts[i], max(1, remaining * loads[i] // whole), surplus)
            counts[i] = counts[i] + extra
            surplus = surplus - extra
    return np.array([most] + counts)


def uneven(key, count, total, most, slope):
    if count == 2:
        one = jax.random.randint(key, (), max(1, total - most), min(most, total - 1) + 1)
        return jnp.stack([one, total - one])
    sizes = jnp.asarray(length_profile(count, total, most, slope), jnp.int32)
    pairs = (count - 1) // 2
    donor, receiver = sizes[1:1 + 2 * pairs:2], sizes[2:2 + 2 * pairs:2]
    slack = jnp.minimum(donor - 1, most - receiver)
    shifted = jax.random.randint(jax.random.fold_in(key, 1), (pairs,), 0, 1 << 20) % (slack + 1)
    sizes = sizes.at[1:1 + 2 * pairs:2].set(donor - shifted).at[2:2 + 2 * pairs:2].set(receiver + shifted)
    return sizes[jax.random.permutation(jax.random.fold_in(key, 2), count)]


def gaussian(rng, extent, deviation, reach, split=(), kind=jnp.bfloat16):
    array = deviation * jax.random.normal(rng, extent, jnp.float32)
    if split:
        array = array * levels(rng, extent, split, -0.22, 0.18)
    return jnp.clip(array, -reach, reach).astype(kind)


def setup_inputs(seed: int = 0) -> dict:
    seeds = jax.random.split(jax.random.key(seed), 9)
    return {
        "events": gaussian(seeds[0], (HIST, LEN, D), 1.0, 6.0, ((0, 4), (1, 8))),
        "w_in": gaussian(seeds[1], (D, 4 * D), D ** -0.5, 0.1875, ((1, 4),)),
        "w_out": gaussian(seeds[2], (D, D), D ** -0.5, 0.1875),
        "item_table": gaussian(seeds[3], (ITEMS, D), 1.0, 6.0, ((0, 32),)),
        "item_bias": jnp.clip(-10.0 + 4.0 * jax.random.uniform(seeds[4], (ITEMS,), jnp.float32) ** levels(seeds[4], (ITEMS,), ((0, 32),), -0.2, 0.2), -10.0, -6.0).astype(jnp.bfloat16),
        "segment_lengths": jax.vmap(lambda own: uneven(own, SEGS, LEN, LEN // 2, 2))(jax.random.split(seeds[5], HIST)).reshape((HIST, SEGS)).astype(jnp.int32),
        "listed_pos": set_ends(jax.random.randint(seeds[6], (LIST_HIST, HIST), 0, LEN), jax.random.fold_in(seeds[6], 1), 0, LEN - 1).astype(jnp.int32),
        "labels": set_ends(jax.random.randint(seeds[7], (LIST_HIST, HIST), 0, ITEMS), jax.random.fold_in(seeds[7], 1), 0, ITEMS - 1).astype(jnp.int32),
    }


def segment_starts(lengths, length):
    ends = jnp.cumsum(lengths, axis=-1).astype(jnp.int32)
    positions = jnp.arange(length, dtype=jnp.int32)
    passed = (positions[:, None] >= ends[..., None, :]).astype(jnp.int32)
    return lax.optimization_barrier(jnp.sum(passed * lengths[..., None, :], axis=-1)).astype(jnp.int32)

def attend_head(query, key, value, start):
    head_size, length = query.shape
    block = min(512, length)
    count = length // block
    query_wide = query.astype(jnp.float32)
    key_wide = key.astype(jnp.float32)
    value_wide = value.astype(jnp.float32)

    def one_block(number, result):
        number = number.astype(jnp.int32)
        rows = number * block + jnp.arange(block, dtype=jnp.int32)
        query_block = lax.dynamic_slice_in_dim(query_wide, number * block, block, 1)
        row_start = lax.dynamic_slice_in_dim(start, number * block, block, 0)

        def add_tile(other, accum):
            other = other.astype(jnp.int32)
            columns = other * block + jnp.arange(block, dtype=jnp.int32)
            key_block = lax.dynamic_slice_in_dim(key_wide, other * block, block, 1)
            value_block = lax.dynamic_slice_in_dim(value_wide, other * block, block, 1)
            scores = jnp.einsum('dq,dk->qk', query_block, key_block)
            allowed = (columns[None, :] <= rows[:, None]) & (columns[None, :] >= row_start[:, None])
            weights = jnp.where(allowed, jax.nn.silu(scores), 0.0).astype(jnp.bfloat16)
            weights = lax.optimization_barrier(weights).astype(jnp.float32)
            return accum + jnp.einsum('qk,dk->dq', weights, value_block)
        first = (row_start[0] // block).astype(jnp.int32)
        accum = lax.fori_loop(first, (number + 1).astype(jnp.int32), add_tile, jnp.zeros((head_size, block), jnp.float32))
        return lax.dynamic_update_slice_in_dim(result, accum, number * block, 1)
    return lax.fori_loop(jnp.int32(0), jnp.int32(count), one_block, jnp.zeros((head_size, length), jnp.float32))

def reference(events, w_in, w_out, item_table, item_bias, segment_lengths, listed_pos, labels):

    def one_history(pair):
        history, lengths = pair
        acts = jax.nn.silu(jnp.dot(history, w_in, preferred_element_type=jnp.float32)).astype(jnp.bfloat16)
        gate_u = acts[:, :D].astype(jnp.float32)

        def split_heads(block_cols):
            return block_cols.reshape(LEN, HEADS, HD).transpose(1, 2, 0)
        values = split_heads(acts[:, D:2 * D])
        queries = split_heads(acts[:, 2 * D:3 * D])
        keys = split_heads(acts[:, 3 * D:])
        start = segment_starts(lengths, LEN)
        attended = lax.map(lambda trio: attend_head(trio[0], trio[1], trio[2], start), (queries, keys, values))
        attended = lax.optimization_barrier(attended.astype(jnp.bfloat16)).astype(jnp.float32)
        attended = attended.transpose(2, 0, 1).reshape(LEN, D)
        center = attended - lax.optimization_barrier(jnp.mean(attended, axis=1, keepdims=True))
        spread = lax.optimization_barrier(jnp.mean(center * center, axis=1, keepdims=True))
        normed = center * lax.rsqrt(spread + 1e-05)
        mixed = (normed * gate_u).astype(jnp.bfloat16)
        output = jnp.dot(mixed, w_out, preferred_element_type=jnp.float32)
        return (history.astype(jnp.float32) + output).astype(jnp.bfloat16)
    layer_out = lax.map(one_history, (events, segment_lengths))
    rows = layer_out[jnp.arange(HIST, dtype=jnp.int32)[None, :], listed_pos].astype(jnp.float32)
    table_blocks = item_table.reshape(ITEMS // IDEV, IDEV, D)
    bias_blocks = item_bias.reshape(ITEMS // IDEV, IDEV)
    scale = D ** (-0.5)

    def add_block(total, part):
        number, table, bias = part
        item_ids = number * IDEV + jnp.arange(IDEV, dtype=jnp.int32)
        table_wide = table.astype(jnp.float32)
        logits = jnp.einsum('lhd,kd->lhk', rows, table_wide) * scale + bias.astype(jnp.float32)
        target = (labels[:, :, None] == item_ids[None, None, :]).astype(jnp.float32)
        coef = (jax.nn.sigmoid(logits) - target).astype(jnp.bfloat16)
        coef = lax.optimization_barrier(coef).astype(jnp.float32)
        return (total + jnp.einsum('lhk,kd->lhd', coef, table_wide), None)
    hidden_grad, _ = lax.scan(add_block, jnp.zeros((LIST_HIST, HIST, D), jnp.float32), (jnp.arange(ITEMS // IDEV, dtype=jnp.int32), table_blocks, bias_blocks))
    return (layer_out, hidden_grad)
```

```python
import functools

import jax
import jax.numpy as jnp
from jax import lax
from jax.experimental import pallas as pl
from jax.experimental.pallas import tpu as pltpu
from jax.sharding import PartitionSpec as P

HEADS = 16
HD = 64
D = 1024
BF = jnp.bfloat16
F32 = jnp.float32
CHUNKS = (256, 256)
PAD = 16
VMEM_LIMIT = 56 * 1024 * 1024


def silu_half(half):
    return half + half * jnp.tanh(half)


def attend_kernel(blocks, split, tag_ref, seg_ref, *refs):
    events = refs[:blocks]
    weights = refs[blocks : blocks + len(split)]
    keep_ref, send_ref, acts, mask, accum = refs[blocks + len(split) :]
    hist, here, width = events[0].shape
    cols = keep_ref.shape[-1]
    flip, place, core = tag_ref[0], tag_ref[1], tag_ref[2]
    chip = 2 * here

    def positions(shape, dim, back):
        at = lax.broadcasted_iota(jnp.int32, shape, dim)
        first = (at < here).astype(jnp.int32)
        rank = first * core + (1 - first) * (1 - core)
        return (place - back) * chip + rank * here + at - (1 - first) * here

    for h in range(hist):
        row = positions((chip, 1), 0, 0)
        start = jnp.zeros((chip, 1), jnp.int32)
        end = jnp.int32(0)
        for k in range(seg_ref.shape[1]):
            end = end + seg_ref[h, k]
            start = start + jnp.where(row >= end, seg_ref[h, k], 0)
        for back in range(blocks // 2):
            col = positions((1, chip), 1, back)
            allowed = (col <= row) & (col >= start)
            mask[h, back] = jnp.where(allowed, 1.0, 0.0).astype(F32)

    def project(slot, block):
        rows = events[block][...].reshape(hist * here, width)
        total, base = None, 0
        for ref, owner in zip(weights, split):
            if owner == slot:
                depth = ref.shape[0]
                part = jnp.dot(rows[:, base : base + depth], ref[...], preferred_element_type=F32)
                total = part if total is None else total + part
                base += depth
        acts[slot, block] = silu_half(0.5 * total).astype(BF).reshape(hist, here, cols)

    for slot in range(4):
        for block in range(2):
            project(slot, block)

        @pl.when(((flip ^ slot) & 1) == 1)
        def _(slot=slot):
            for block in range(2, blocks):
                project(slot, block)

    gate, value, query, key = flip, flip ^ 1, flip ^ 2, flip ^ 3
    keep_ref[1] = acts[gate, 0]
    send_ref[1] = acts[gate, 1]
    lane = lax.broadcasted_iota(jnp.int32, (1, 128), 1)
    low = (lane < HD).astype(BF)
    high = 1 - low
    for h in range(hist):
        accum[...] = jnp.zeros_like(accum)
        first_row = place * chip
        first_start, end = jnp.int32(0), jnp.int32(0)
        for k in range(seg_ref.shape[1]):
            end = end + seg_ref[h, k]
            first_start = first_start + jnp.where(first_row >= end, seg_ref[h, k], 0)
        for back in range(blocks // 2):

            @pl.when(first_start < (place - back + 1) * chip)
            def _(h=h, back=back):
                allowed = mask[h, back]
                for pair in range(cols // 128):
                    at = slice(pair * 128, pair * 128 + 128)
                    q = jnp.concatenate([acts[query, 0, h, :, at], acts[query, 1, h, :, at]], 0)
                    k = jnp.concatenate(
                        [acts[key, 2 * back, h, :, at], acts[key, 2 * back + 1, h, :, at]], 0
                    )
                    v = jnp.concatenate(
                        [acts[value, 2 * back, h, :, at], acts[value, 2 * back + 1, h, :, at]], 0
                    )
                    q = q * jnp.asarray(0.5, BF)
                    total = accum[:, at]
                    for lanes in (low, high):
                        half = lax.dot_general(
                            q * lanes, k, (((1,), (1,)), ((), ())), preferred_element_type=F32
                        )
                        w = silu_half(half * allowed).astype(BF)
                        total = total + jnp.dot(w, v * lanes, preferred_element_type=F32)
                    accum[:, at] = total

        keep_ref[0, h] = accum[:here].astype(BF)
        send_ref[0, h] = accum[here:].astype(BF)


def attend(tag, lengths, events, weights, split, cols):
    hist, here, width = events[0].shape
    blocks = len(events)
    part = jax.ShapeDtypeStruct((2, hist, here, cols), BF)
    vmem = pl.BlockSpec(memory_space=pltpu.VMEM)
    smem = pl.BlockSpec(memory_space=pltpu.SMEM)
    flops = 2 * hist * here * width * cols * (2 * blocks + 4) + 8 * hist * 2 * here * here * blocks * cols
    return pl.pallas_call(
        functools.partial(attend_kernel, blocks, split),
        out_shape=(part, part),
        in_specs=[smem, smem] + [vmem] * (blocks + len(weights)),
        out_specs=(vmem, vmem),
        scratch_shapes=[
            pltpu.VMEM((4, blocks, hist, here, cols), BF),
            pltpu.VMEM((hist, blocks // 2, 2 * here, 2 * here), F32),
            pltpu.VMEM((2 * here, cols), F32),
        ],
        compiler_params=pltpu.CompilerParams(vmem_limit_bytes=VMEM_LIMIT),
        cost_estimate=pl.CostEstimate(
            flops=flops, bytes_accessed=4 * 1024 * 1024, transcendentals=hist * here * 2 * here * blocks * cols // HD
        ),
        name="attend",
    )(tag, lengths, *events, *weights)


def finish_kernel(count, tag_ref, listed_ref, events_ref, w_out_ref, *refs):
    parts = refs[: 2 * count]
    layer_ref, keep_ref, send_ref = refs[2 * count :]
    hist, here, width = events_ref.shape
    rows = hist * here
    core = tag_ref[2]
    pieces, gates, offsets = [], [], []
    for side in range(2):
        base = (core ^ side) * (width // 2)
        for ref in parts[side * count : (side + 1) * count]:
            cols = ref.shape[-1]
            pieces.append(ref[0].reshape(rows, cols).astype(F32))
            gates.append(ref[1].reshape(rows, cols).astype(F32))
            offsets.append(pl.multiple_of(base, 128))
            base = base + cols
    mean = sum(jnp.sum(p, axis=1, keepdims=True) for p in pieces) * (1.0 / width)
    pieces = [p - mean for p in pieces]
    spread = sum(jnp.sum(p * p, axis=1, keepdims=True) for p in pieces) * (1.0 / width)
    inverse = lax.rsqrt(spread + 1e-05)
    output = events_ref[...].reshape(rows, width).astype(F32)
    for p, g, at in zip(pieces, gates, offsets):
        mixed = (p * inverse * g).astype(BF)
        output = output + jnp.dot(
            mixed, w_out_ref[pl.ds(at, p.shape[1]), :], preferred_element_type=F32
        )
    layer = output.astype(BF)
    layer_ref[...] = layer.reshape(hist, here, width)
    column = lax.broadcasted_iota(jnp.int32, (1, rows), 1)
    for side, out_ref in ((0, keep_ref), (1, send_ref)):
        pick = (listed_ref[side] == column).astype(BF)
        out_ref[...] = jnp.dot(pick, layer, preferred_element_type=F32).astype(BF)


def finish(tag, listed, events, w_out, keeps, received):
    hist, here, width = events.shape
    rows = listed.shape[1]
    vmem = pl.BlockSpec(memory_space=pltpu.VMEM)
    smem = pl.BlockSpec(memory_space=pltpu.SMEM)
    return pl.pallas_call(
        functools.partial(finish_kernel, len(keeps)),
        out_shape=(
            jax.ShapeDtypeStruct((hist, here, width), BF),
            jax.ShapeDtypeStruct((rows, width), BF),
            jax.ShapeDtypeStruct((rows, width), BF),
        ),
        in_specs=[smem] + [vmem] * (3 + len(keeps) + len(received)),
        out_specs=(vmem, vmem, vmem),
        compiler_params=pltpu.CompilerParams(vmem_limit_bytes=VMEM_LIMIT),
        cost_estimate=pl.CostEstimate(
            flops=2 * hist * here * width * width, bytes_accessed=5 * 1024 * 1024, transcendentals=0
        ),
        name="finish",
    )(tag, listed, events, w_out, *keeps, *received)


def score_kernel(sources, tag_ref, base_ref, rows_ref, label_ref, *refs):
    tables = refs[:sources]
    outs = refs[sources:-2]
    total, shares = refs[-2:]
    rows = rows_ref[...]
    label = label_ref[...]
    scale = D ** (-0.5)
    total[...] = jnp.zeros_like(total)
    which = 0
    for ref in tables:
        per = ref.shape[0]
        items = ref.shape[1] - PAD

        def one(i, which=which, ref=ref, items=items):
            table = ref[i, :items, :]
            bias = ref[i, items : items + 1, :items].astype(F32)
            logits = lax.dot_general(
                rows, table, (((1,), (1,)), ((), ())), preferred_element_type=F32
            )
            logits = logits * scale + bias
            ids = base_ref[which + i] + lax.broadcasted_iota(jnp.int32, (1, items), 1)
            target = (label == ids).astype(F32)
            coef = (1.0 / (1.0 + jnp.exp(-logits)) - target).astype(BF)
            total[...] += jnp.dot(coef, table, preferred_element_type=F32)

        if per <= 4:
            for i in range(per):
                one(i)
        else:
            pl.loop(0, per)(one)
        which += per
    count = len(outs)
    share = outs[0].shape[0]
    for chip in range(count):
        shares[chip] = total[chip * share : (chip + 1) * share, :]
    for step, out in enumerate(outs):
        out[...] = shares[lax.rem(tag_ref[1] + step, count)]


def score(tag, bases, rows, labels, tables, chips):
    count, width = rows.shape
    vmem = pl.BlockSpec(memory_space=pltpu.VMEM)
    smem = pl.BlockSpec(memory_space=pltpu.SMEM)
    part = jax.ShapeDtypeStruct((count // chips, width), F32)
    return pl.pallas_call(
        functools.partial(score_kernel, len(tables)),
        out_shape=(part,) * chips,
        in_specs=[smem, smem] + [vmem] * (2 + len(tables)),
        out_specs=(vmem,) * chips,
        scratch_shapes=[
            pltpu.VMEM((count, width), F32),
            pltpu.VMEM((chips, count // chips, width), F32),
        ],
        compiler_params=pltpu.CompilerParams(vmem_limit_bytes=VMEM_LIMIT),
        cost_estimate=pl.CostEstimate(
            flops=4 * count * width * 1024, bytes_accessed=3 * 1024 * 1024, transcendentals=count * 1024
        ),
        name="score",
    )(tag, bases, rows, labels, *tables)


def on_device(events, w_in, w_out, item_table, item_bias, segment_lengths, listed_pos, labels):
    hist, here, width = events.shape
    seq = lax.axis_size("seq")
    batch = lax.axis_size("batch")
    chips = seq // 2
    rank = lax.axis_index("seq").astype(jnp.int32)
    mine = lax.axis_index("batch").astype(jnp.int32)
    place, core = rank // 2, rank % 2
    grid = batch == 4

    def swap(value):
        return lax.ppermute(value, "seq", [(i, i ^ 1) for i in range(seq)])

    def across(value, bit):
        return lax.ppermute(value, "batch", [(i, i ^ bit) for i in range(batch)])

    def ahead(value, by):
        return lax.ppermute(value, "seq", [(i, i + 2 * by) for i in range(seq - 2 * by)])

    half = width // 2
    chunks = []
    if grid:
        offset = core * half
        for cols in CHUNKS:
            own = lax.dynamic_slice_in_dim(w_in, offset, cols, 1)
            over_x, over_y = across(own, 1), across(own, 2)
            top = across(over_y[: width // 2], 1)
            bottom = across(over_x[width // 2 :], 2)
            chunks.append(([own, over_x, over_y, top, bottom], (0, 1, 2, 3, 3)))
            offset = offset + cols
        flip = mine
    else:
        whole = lax.all_gather(w_in, "batch", axis=1, tiled=True)
        offset = core * half
        for cols in CHUNKS:
            chunks.append(
                (
                    [
                        lax.dynamic_slice_in_dim(whole, group * width + offset, cols, 1)
                        for group in range(4)
                    ],
                    (0, 1, 2, 3),
                )
            )
            offset = offset + cols
        flip = jnp.int32(0)

    longest = seq * here // 2
    reach = min(chips - 1, -(-(longest - 1) // (2 * here)))
    blocks = [events, swap(events)]
    for back in range(1, reach + 1):
        earlier = ahead(events, back)
        blocks += [earlier, swap(earlier)]

    tag = jnp.stack([flip, place, core])
    keeps, received = [], []
    for (weights, split), cols in zip(chunks, CHUNKS):
        keep, send = attend(tag, segment_lengths, blocks, weights, split, cols)
        keeps.append(keep)
        received.append(swap(send))

    share = listed_pos.shape[0] // seq
    local = listed_pos - rank * here
    inside = (local >= 0) & (local < here)
    index = jnp.where(inside, local + here * jnp.arange(hist, dtype=jnp.int32)[None, :], -1)

    def halves(value):
        value = value.reshape(chips, 2, share, hist).transpose(1, 0, 2, 3)
        return value.reshape(2, chips * share * hist, 1)

    index = halves(index)
    index = jnp.where(core == 0, index, index[::-1])
    own_labels = halves(labels)
    own_labels = jnp.where(core == 0, own_labels[0], own_labels[1])
    layer_out, rows, rows_send = finish(tag, index, events, w_out, keeps, received)
    rows = rows + swap(rows_send)
    step = 1
    while step < chips:
        rows = rows + lax.ppermute(rows, "seq", [(i, i ^ (2 * step)) for i in range(seq)])
        step *= 2

    items = item_table.shape[0]
    padded = jnp.concatenate(
        [
            item_table,
            jnp.pad(item_bias[None, :], ((0, PAD - 1), (0, width - items))),
        ],
        0,
    )
    if grid:
        over_x = across(padded, 1)
        over_y = across(padded, 2)
        corner = across(padded, 3)
        table = jnp.stack([padded, over_x, over_y, corner])
        holder = mine ^ jnp.arange(4, dtype=jnp.int32)
    else:
        table = lax.all_gather(padded[None], "batch", axis=0, tiled=True)
        holder = jnp.arange(batch, dtype=jnp.int32)
    other_table = swap(table)
    bases = jnp.concatenate(
        [(rank * batch + holder) * items, ((rank ^ 1) * batch + holder) * items]
    )
    parts = score(tag, bases, rows, own_labels, (table, other_table), chips)
    total = parts[0]
    for step in range(1, chips):
        total = total + lax.ppermute(
            parts[step], "seq", [(i, (i + 2 * step) % seq) for i in range(seq)]
        )
    return layer_out, total.reshape(share, hist, width)


def solution(mesh):
    return jax.shard_map(
        on_device,
        mesh=mesh,
        in_specs=(
            P("batch", "seq", None),
            P(None, "batch"),
            P(),
            P(("seq", "batch"), None),
            P(("seq", "batch")),
            P("batch", None),
            P(None, "batch"),
            P(None, "batch"),
        ),
        out_specs=(P("batch", "seq", None), P("seq", "batch", None)),
        check_vma=False,
    )
```

```python
import functools

import jax
import jax.numpy as jnp
from jax import lax
from jax.experimental import pallas as pl
from jax.experimental.pallas import tpu as pltpu
from jax.sharding import PartitionSpec as P

HEADS = 16
HD = 64
D = 1024
BF = jnp.bfloat16
F32 = jnp.float32
CHUNKS = (384, 128)
PAD = 16
MIB = 1024 * 1024


def silu_half(half):
    return half + half * jnp.tanh(half)


def attend_kernel(blocks, split, tag_ref, seg_ref, *refs):
    events = refs[:blocks]
    weights = refs[blocks : blocks + len(split)]
    keep_ref, send_ref, acts, mask, accum = refs[blocks + len(split) :]
    hist, here, width = events[0].shape
    cols = keep_ref.shape[-1]
    flip, place, core = tag_ref[0], tag_ref[1], tag_ref[2]
    chip = 2 * here

    def positions(shape, dim, back):
        at = lax.broadcasted_iota(jnp.int32, shape, dim)
        first = (at < here).astype(jnp.int32)
        rank = first * core + (1 - first) * (1 - core)
        return (place - back) * chip + rank * here + at - (1 - first) * here

    for h in range(hist):
        row = positions((chip, 1), 0, 0)
        start = jnp.zeros((chip, 1), jnp.int32)
        end = jnp.int32(0)
        for k in range(seg_ref.shape[1]):
            end = end + seg_ref[h, k]
            start = start + jnp.where(row >= end, seg_ref[h, k], 0)
        for back in range(blocks // 2):
            col = positions((1, chip), 1, back)
            allowed = (col <= row) & (col >= start)
            mask[h, back] = jnp.where(allowed, 1.0, 0.0).astype(F32)

    def project(slot, block):
        rows = events[block][...].reshape(hist * here, width)
        total, base = None, 0
        for ref, owner in zip(weights, split):
            if owner == slot:
                depth = ref.shape[0]
                part = jnp.dot(rows[:, base : base + depth], ref[...], preferred_element_type=F32)
                total = part if total is None else total + part
                base += depth
        acts[slot, block] = silu_half(0.5 * total).astype(BF).reshape(hist, here, cols)

    for slot in range(4):
        for block in range(2):
            project(slot, block)

        @pl.when(((flip ^ slot) & 1) == 1)
        def _(slot=slot):
            for block in range(2, blocks):
                project(slot, block)

    gate, value, query, key = flip, flip ^ 1, flip ^ 2, flip ^ 3
    keep_ref[1] = acts[gate, 0]
    send_ref[1] = acts[gate, 1]
    lane = lax.broadcasted_iota(jnp.int32, (1, 128), 1)
    low = (lane < HD).astype(BF)
    high = 1 - low
    for h in range(hist):
        accum[...] = jnp.zeros_like(accum)
        first_row = place * chip
        first_start, end = jnp.int32(0), jnp.int32(0)
        for k in range(seg_ref.shape[1]):
            end = end + seg_ref[h, k]
            first_start = first_start + jnp.where(first_row >= end, seg_ref[h, k], 0)
        for back in range(blocks // 2):

            @pl.when(first_start < (place - back + 1) * chip)
            def _(h=h, back=back):
                allowed = mask[h, back]
                for pair in range(cols // 128):
                    at = slice(pair * 128, pair * 128 + 128)
                    q = jnp.concatenate([acts[query, 0, h, :, at], acts[query, 1, h, :, at]], 0)
                    k = jnp.concatenate(
                        [acts[key, 2 * back, h, :, at], acts[key, 2 * back + 1, h, :, at]], 0
                    )
                    v = jnp.concatenate(
                        [acts[value, 2 * back, h, :, at], acts[value, 2 * back + 1, h, :, at]], 0
                    )
                    q = q * jnp.asarray(0.5, BF)
                    total = accum[:, at]
                    for lanes in (low, high):
                        half = lax.dot_general(
                            q * lanes, k, (((1,), (1,)), ((), ())), preferred_element_type=F32
                        )
                        w = silu_half(half * allowed).astype(BF)
                        total = total + jnp.dot(w, v * lanes, preferred_element_type=F32)
                    accum[:, at] = total

        keep_ref[0, h] = accum[:here].astype(BF)
        send_ref[0, h] = accum[here:].astype(BF)


def attend(tag, lengths, events, weights, split, cols):
    hist, here, width = events[0].shape
    blocks = len(events)
    part = jax.ShapeDtypeStruct((2, hist, here, cols), BF)
    vmem = pl.BlockSpec(memory_space=pltpu.VMEM)
    smem = pl.BlockSpec(memory_space=pltpu.SMEM)
    flops = 2 * hist * here * width * cols * (2 * blocks + 4) + 8 * hist * 2 * here * here * blocks * cols
    return pl.pallas_call(
        functools.partial(attend_kernel, blocks, split),
        out_shape=(part, part),
        in_specs=[smem, smem] + [vmem] * (blocks + len(weights)),
        out_specs=(vmem, vmem),
        scratch_shapes=[
            pltpu.VMEM((4, blocks, hist, here, cols), BF),
            pltpu.VMEM((hist, blocks // 2, 2 * here, 2 * here), F32),
            pltpu.VMEM((2 * here, cols), F32),
        ],
        compiler_params=pltpu.CompilerParams(vmem_limit_bytes=(8 + 2 * blocks) * MIB),
        cost_estimate=pl.CostEstimate(
            flops=flops, bytes_accessed=4 * 1024 * 1024, transcendentals=hist * here * 2 * here * blocks * cols // HD
        ),
        name="attend",
    )(tag, lengths, *events, *weights)


def finish_kernel(count, tag_ref, listed_ref, events_ref, w_out_ref, *refs):
    parts = refs[: 2 * count]
    layer_ref, keep_ref, send_ref = refs[2 * count :]
    hist, here, width = events_ref.shape
    rows = hist * here
    core = tag_ref[2]
    pieces, gates, offsets = [], [], []
    for side in range(2):
        base = (core ^ side) * (width // 2)
        for ref in parts[side * count : (side + 1) * count]:
            cols = ref.shape[-1]
            pieces.append(ref[0].reshape(rows, cols).astype(F32))
            gates.append(ref[1].reshape(rows, cols).astype(F32))
            offsets.append(pl.multiple_of(base, 128))
            base = base + cols
    mean = sum(jnp.sum(p, axis=1, keepdims=True) for p in pieces) * (1.0 / width)
    pieces = [p - mean for p in pieces]
    spread = sum(jnp.sum(p * p, axis=1, keepdims=True) for p in pieces) * (1.0 / width)
    inverse = lax.rsqrt(spread + 1e-05)
    output = events_ref[...].reshape(rows, width).astype(F32)
    for p, g, at in zip(pieces, gates, offsets):
        mixed = (p * inverse * g).astype(BF)
        output = output + jnp.dot(
            mixed, w_out_ref[pl.ds(at, p.shape[1]), :], preferred_element_type=F32
        )
    layer = output.astype(BF)
    layer_ref[...] = layer.reshape(hist, here, width)
    column = lax.broadcasted_iota(jnp.int32, (1, rows), 1)
    for side, out_ref in ((0, keep_ref), (1, send_ref)):
        pick = (listed_ref[side] == column).astype(BF)
        out_ref[...] = jnp.dot(pick, layer, preferred_element_type=F32).astype(BF)


def finish(tag, listed, events, w_out, keeps, received):
    hist, here, width = events.shape
    rows = listed.shape[1]
    vmem = pl.BlockSpec(memory_space=pltpu.VMEM)
    smem = pl.BlockSpec(memory_space=pltpu.SMEM)
    return pl.pallas_call(
        functools.partial(finish_kernel, len(keeps)),
        out_shape=(
            jax.ShapeDtypeStruct((hist, here, width), BF),
            jax.ShapeDtypeStruct((rows, width), BF),
            jax.ShapeDtypeStruct((rows, width), BF),
        ),
        in_specs=[smem] + [vmem] * (3 + len(keeps) + len(received)),
        out_specs=(vmem, vmem, vmem),
        compiler_params=pltpu.CompilerParams(vmem_limit_bytes=16 * MIB),
        cost_estimate=pl.CostEstimate(
            flops=2 * hist * here * width * width, bytes_accessed=5 * 1024 * 1024, transcendentals=0
        ),
        name="finish",
    )(tag, listed, events, w_out, *keeps, *received)


def score_kernel(sources, tag_ref, base_ref, rows_ref, label_ref, *refs):
    tables = refs[:sources]
    outs = refs[sources:-2]
    total, shares = refs[-2:]
    rows = rows_ref[...]
    label = label_ref[...]
    scale = D ** (-0.5)
    total[...] = jnp.zeros_like(total)
    which = 0
    for ref in tables:
        per = ref.shape[0]
        items = ref.shape[1] - PAD

        def one(i, which=which, ref=ref, items=items):
            table = ref[i, :items, :]
            bias = ref[i, items : items + 1, :items].astype(F32)
            logits = lax.dot_general(
                rows, table, (((1,), (1,)), ((), ())), preferred_element_type=F32
            )
            logits = logits * scale + bias
            ids = base_ref[which + i] + lax.broadcasted_iota(jnp.int32, (1, items), 1)
            target = (label == ids).astype(F32)
            coef = (1.0 / (1.0 + jnp.exp(-logits)) - target).astype(BF)
            total[...] += jnp.dot(coef, table, preferred_element_type=F32)

        if per <= 4:
            for i in range(per):
                one(i)
        else:
            pl.loop(0, per)(one)
        which += per
    count = len(outs)
    share = outs[0].shape[0]
    for chip in range(count):
        shares[chip] = total[chip * share : (chip + 1) * share, :]
    for step, out in enumerate(outs):
        out[...] = shares[lax.rem(tag_ref[1] + step, count)]


def score(tag, bases, rows, labels, tables, chips):
    count, width = rows.shape
    vmem = pl.BlockSpec(memory_space=pltpu.VMEM)
    smem = pl.BlockSpec(memory_space=pltpu.SMEM)
    part = jax.ShapeDtypeStruct((count // chips, width), F32)
    return pl.pallas_call(
        functools.partial(score_kernel, len(tables)),
        out_shape=(part,) * chips,
        in_specs=[smem, smem] + [vmem] * (2 + len(tables)),
        out_specs=(vmem,) * chips,
        scratch_shapes=[
            pltpu.VMEM((count, width), F32),
            pltpu.VMEM((chips, count // chips, width), F32),
        ],
        compiler_params=pltpu.CompilerParams(vmem_limit_bytes=8 * MIB + 3 * sum(t.size for t in tables)),
        cost_estimate=pl.CostEstimate(
            flops=4 * count * width * 1024, bytes_accessed=3 * 1024 * 1024, transcendentals=count * 1024
        ),
        name="score",
    )(tag, bases, rows, labels, *tables)


def on_device(events, w_in, w_out, item_table, item_bias, segment_lengths, listed_pos, labels):
    hist, here, width = events.shape
    seq = lax.axis_size("seq")
    batch = lax.axis_size("batch")
    chips = seq // 2
    rank = lax.axis_index("seq").astype(jnp.int32)
    mine = lax.axis_index("batch").astype(jnp.int32)
    place, core = rank // 2, rank % 2
    grid = batch == 4

    def swap(value):
        return lax.ppermute(value, "seq", [(i, i ^ 1) for i in range(seq)])

    def across(value, bit):
        return lax.ppermute(value, "batch", [(i, i ^ bit) for i in range(batch)])

    def ahead(value, by):
        return lax.ppermute(value, "seq", [(i, i + 2 * by) for i in range(seq - 2 * by)])

    half = width // 2
    chunks = []
    offset = core * half
    if grid:
        first = []
        for cols in CHUNKS:
            own = lax.dynamic_slice_in_dim(w_in, offset, cols, 1)
            offset = offset + cols
            if not chunks:
                over_x, over_y = across(own, 1), across(own, 2)
                first = [own, over_x, over_y]
                top = across(over_y[: width // 2], 1)
                bottom = across(over_x[width // 2 :], 2)
                chunks.append((first + [top, bottom], (0, 1, 2, 3, 3)))
            else:
                own, _ = lax.optimization_barrier((own, chunks[0][0]))
                chunks.append(([own] + [across(own, bit) for bit in (1, 2, 3)], (0, 1, 2, 3)))
        flip = mine
    else:
        whole = lax.all_gather(w_in, "batch", axis=1, tiled=True)
        for cols in CHUNKS:
            groups = [
                lax.dynamic_slice_in_dim(whole, group * width + offset, cols, 1)
                for group in range(4)
            ]
            chunks.append((groups, (0, 1, 2, 3)))
            offset = offset + cols
        flip = jnp.int32(0)

    longest = seq * here // 2
    reach = min(chips - 1, -(-(longest - 1) // (2 * here)))
    window = [events]
    for back in range(reach):
        last = window[-1]
        if grid and back == 0:
            last, _ = lax.optimization_barrier((last, first[0]))
        elif grid and back == 1:
            last, _ = lax.optimization_barrier((last, first))
        window.append(ahead(last, 1))
    blocks = []
    for back, block in enumerate(window):
        source = block
        if back == 0:
            source, _ = lax.optimization_barrier((block, window[1]))
        elif grid and back == reach:
            source, _ = lax.optimization_barrier((block, chunks[0][0]))
        blocks += [block, swap(source)]

    tag = jnp.stack([flip, place, core])
    keeps, received = [], []
    for (weights, split), cols in zip(chunks, CHUNKS):
        keep, send = attend(tag, segment_lengths, blocks, weights, split, cols)
        keeps.append(keep)
        received.append(swap(send))

    share = listed_pos.shape[0] // seq
    local = listed_pos - rank * here
    inside = (local >= 0) & (local < here)
    index = jnp.where(inside, local + here * jnp.arange(hist, dtype=jnp.int32)[None, :], -1)

    def halves(value):
        value = value.reshape(chips, 2, share, hist).transpose(1, 0, 2, 3)
        return value.reshape(2, chips * share * hist, 1)

    index = halves(index)
    index = jnp.where(core == 0, index, index[::-1])
    own_labels = halves(labels)
    own_labels = jnp.where(core == 0, own_labels[0], own_labels[1])
    layer_out, rows, rows_send = finish(tag, index, events, w_out, keeps, received)
    rows = rows + swap(rows_send)
    step = 1
    while step < chips:
        rows = rows + lax.ppermute(rows, "seq", [(i, i ^ (2 * step)) for i in range(seq)])
        step *= 2

    items = item_table.shape[0]
    item_table, _ = lax.optimization_barrier((item_table, (chunks[-1][0], keeps[0])))
    padded = jnp.concatenate(
        [
            item_table,
            jnp.pad(item_bias[None, :], ((0, PAD - 1), (0, width - items))),
        ],
        0,
    )
    if grid:
        over_x = across(padded, 1)
        over_y = across(padded, 2)
        corner = across(padded, 3)
        over_x, over_y, corner, _ = lax.optimization_barrier((over_x, over_y, corner, rows_send))
        table = jnp.stack([padded, over_x, over_y, corner])
        holder = mine ^ jnp.arange(4, dtype=jnp.int32)
    else:
        table = lax.all_gather(padded[None], "batch", axis=0, tiled=True)
        holder = jnp.arange(batch, dtype=jnp.int32)
    other_table = swap(table)
    bases = jnp.concatenate(
        [(rank * batch + holder) * items, ((rank ^ 1) * batch + holder) * items]
    )
    parts = score(tag, bases, rows, own_labels, (table, other_table), chips)
    total = parts[0]
    for step in range(1, chips):
        total = total + lax.ppermute(
            parts[step], "seq", [(i, (i + 2 * step) % seq) for i in range(seq)]
        )
    return layer_out, total.reshape(share, hist, width)


def solution(mesh):
    return jax.shard_map(
        on_device,
        mesh=mesh,
        in_specs=(
            P("batch", "seq", None),
            P(None, "batch"),
            P(),
            P(("seq", "batch"), None),
            P(("seq", "batch")),
            P("batch", None),
            P(None, "batch"),
            P(None, "batch"),
        ),
        out_specs=(P("batch", "seq", None), P("seq", "batch", None)),
        check_vma=False,
    )
```

```python
import functools

import jax
import jax.numpy as jnp
from jax import lax
from jax.experimental import pallas as pl
from jax.experimental.pallas import tpu as pltpu
from jax.sharding import PartitionSpec as P

HEADS = 16
HD = 64
D = 1024
BF = jnp.bfloat16
F32 = jnp.float32
CHUNKS = (512,)
PAD = 16
MIB = 1024 * 1024


def silu_half(half):
    return half + half * jnp.tanh(half)


def attend_kernel(blocks, split, tag_ref, seg_ref, *refs):
    sources = refs[:blocks]
    pieces = refs[blocks : blocks + len(split)]
    keep_ref, send_ref, events, weights, acts, mask, accum, event_sem, weight_sem = refs[blocks + len(split) :]
    _, hist, here, width = events.shape
    cols = keep_ref.shape[-1]
    flip, place, core = tag_ref[0], tag_ref[1], tag_ref[2]
    chip = 2 * here

    bases, seen = [], {}
    for ref, slot in zip(pieces, split):
        bases.append(seen.get(slot, 0))
        seen[slot] = bases[-1] + ref.shape[0]

    def event_copy(block):
        return pltpu.make_async_copy(sources[block], events.at[block], event_sem.at[block])

    def weight_copy(at):
        rows = pl.ds(bases[at], pieces[at].shape[0])
        return pltpu.make_async_copy(pieces[at], weights.at[split[at], rows], weight_sem.at[at])

    event_copy(0).start()
    weight_copy(0).start()
    event_copy(1).start()
    for at in range(1, len(split)):
        weight_copy(at).start()
    for block in range(2, blocks):
        event_copy(block).start()

    def positions(shape, dim, back):
        at = lax.broadcasted_iota(jnp.int32, shape, dim)
        first = (at < here).astype(jnp.int32)
        rank = first * core + (1 - first) * (1 - core)
        return (place - back) * chip + rank * here + at - (1 - first) * here

    for h in range(hist):
        row = positions((chip, 1), 0, 0)
        start = jnp.zeros((chip, 1), jnp.int32)
        end = jnp.int32(0)
        for k in range(seg_ref.shape[1]):
            end = end + seg_ref[h, k]
            start = start + jnp.where(row >= end, seg_ref[h, k], 0)
        for back in range(blocks // 2):
            col = positions((1, chip), 1, back)
            allowed = (col <= row) & (col >= start)
            mask[h, back] = jnp.where(allowed, 1.0, 0.0).astype(F32)

    def project(slot, block):
        rows = events[block].reshape(hist * here, width)
        total = jnp.dot(rows, weights[slot], preferred_element_type=F32)
        acts[slot, block] = silu_half(0.5 * total).astype(BF).reshape(hist, here, cols)

    for slot in range(4):
        for at, owner in enumerate(split):
            if owner == slot:
                weight_copy(at).wait()
        for block in range(2):
            if slot == 0:
                event_copy(block).wait()
            project(slot, block)
    for block in range(2, blocks):
        event_copy(block).wait()
    for slot in range(4):

        @pl.when(((flip ^ slot) & 1) == 1)
        def _(slot=slot):
            for block in range(2, blocks):
                project(slot, block)

    gate, value, query, key = flip, flip ^ 1, flip ^ 2, flip ^ 3
    keep_ref[1] = acts[gate, 0]
    send_ref[1] = acts[gate, 1]
    lane = lax.broadcasted_iota(jnp.int32, (1, 128), 1)
    low = (lane < HD).astype(BF)
    high = 1 - low
    for h in range(hist):
        accum[...] = jnp.zeros_like(accum)
        first_row = place * chip
        first_start, end = jnp.int32(0), jnp.int32(0)
        for k in range(seg_ref.shape[1]):
            end = end + seg_ref[h, k]
            first_start = first_start + jnp.where(first_row >= end, seg_ref[h, k], 0)
        for back in range(blocks // 2):

            @pl.when(first_start < (place - back + 1) * chip)
            def _(h=h, back=back):
                allowed = mask[h, back]
                for pair in range(cols // 128):
                    at = slice(pair * 128, pair * 128 + 128)
                    q = jnp.concatenate([acts[query, 0, h, :, at], acts[query, 1, h, :, at]], 0)
                    k = jnp.concatenate(
                        [acts[key, 2 * back, h, :, at], acts[key, 2 * back + 1, h, :, at]], 0
                    )
                    v = jnp.concatenate(
                        [acts[value, 2 * back, h, :, at], acts[value, 2 * back + 1, h, :, at]], 0
                    )
                    q = q * jnp.asarray(0.5, BF)
                    total = accum[:, at]
                    for lanes in (low, high):
                        half = lax.dot_general(
                            q * lanes, k, (((1,), (1,)), ((), ())), preferred_element_type=F32
                        )
                        w = silu_half(half * allowed).astype(BF)
                        total = total + jnp.dot(w, v * lanes, preferred_element_type=F32)
                    accum[:, at] = total

        keep_ref[0, h] = accum[:here].astype(BF)
        send_ref[0, h] = accum[here:].astype(BF)


def attend(tag, lengths, events, weights, split, cols):
    hist, here, width = events[0].shape
    blocks = len(events)
    part = jax.ShapeDtypeStruct((2, hist, here, cols), BF)
    vmem = pl.BlockSpec(memory_space=pltpu.VMEM)
    smem = pl.BlockSpec(memory_space=pltpu.SMEM)
    flops = 2 * hist * here * width * cols * (2 * blocks + 4) + 8 * hist * 2 * here * here * blocks * cols
    return pl.pallas_call(
        functools.partial(attend_kernel, blocks, split),
        out_shape=(part, part),
        in_specs=[smem, smem] + [pl.BlockSpec(memory_space=pltpu.HBM)] * (blocks + len(weights)),
        out_specs=(vmem, vmem),
        scratch_shapes=[
            pltpu.VMEM((blocks, hist, here, width), BF),
            pltpu.VMEM((4, width, cols), BF),
            pltpu.VMEM((4, blocks, hist, here, cols), BF),
            pltpu.VMEM((hist, blocks // 2, 2 * here, 2 * here), F32),
            pltpu.VMEM((2 * here, cols), F32),
            pltpu.SemaphoreType.DMA((blocks,)),
            pltpu.SemaphoreType.DMA((len(split),)),
        ],
        compiler_params=pltpu.CompilerParams(vmem_limit_bytes=60 * MIB),
        cost_estimate=pl.CostEstimate(
            flops=flops, bytes_accessed=4 * 1024 * 1024, transcendentals=hist * here * 2 * here * blocks * cols // HD
        ),
        name="attend",
    )(tag, lengths, *events, *weights)


def finish_kernel(count, tag_ref, listed_ref, events_ref, w_out_ref, *refs):
    parts = refs[: 2 * count]
    layer_ref, keep_ref, send_ref, matrix, matrix_sem = refs[2 * count :]
    copy = pltpu.make_async_copy(w_out_ref, matrix, matrix_sem)
    copy.start()
    hist, here, width = events_ref.shape
    rows = hist * here
    core = tag_ref[2]
    pieces, gates, offsets = [], [], []
    for side in range(2):
        base = (core ^ side) * (width // 2)
        for ref in parts[side * count : (side + 1) * count]:
            cols = ref.shape[-1]
            pieces.append(ref[0].reshape(rows, cols).astype(F32))
            gates.append(ref[1].reshape(rows, cols).astype(F32))
            offsets.append(pl.multiple_of(base, 128))
            base = base + cols
    mean = sum(jnp.sum(p, axis=1, keepdims=True) for p in pieces) * (1.0 / width)
    pieces = [p - mean for p in pieces]
    spread = sum(jnp.sum(p * p, axis=1, keepdims=True) for p in pieces) * (1.0 / width)
    inverse = lax.rsqrt(spread + 1e-05)
    output = events_ref[...].reshape(rows, width).astype(F32)
    copy.wait()
    for p, g, at in zip(pieces, gates, offsets):
        mixed = (p * inverse * g).astype(BF)
        output = output + jnp.dot(
            mixed, matrix[pl.ds(at, p.shape[1]), :], preferred_element_type=F32
        )
    layer = output.astype(BF)
    layer_ref[...] = layer.reshape(hist, here, width)
    column = lax.broadcasted_iota(jnp.int32, (1, rows), 1)
    for side, out_ref in ((0, keep_ref), (1, send_ref)):
        pick = (listed_ref[side] == column).astype(BF)
        out_ref[...] = jnp.dot(pick, layer, preferred_element_type=F32).astype(BF)


def finish(tag, listed, events, w_out, keeps, received):
    hist, here, width = events.shape
    rows = listed.shape[1]
    vmem = pl.BlockSpec(memory_space=pltpu.VMEM)
    smem = pl.BlockSpec(memory_space=pltpu.SMEM)
    return pl.pallas_call(
        functools.partial(finish_kernel, len(keeps)),
        out_shape=(
            jax.ShapeDtypeStruct((hist, here, width), BF),
            jax.ShapeDtypeStruct((rows, width), BF),
            jax.ShapeDtypeStruct((rows, width), BF),
        ),
        in_specs=[smem, vmem, vmem, pl.BlockSpec(memory_space=pltpu.HBM)] + [vmem] * (len(keeps) + len(received)),
        out_specs=(vmem, vmem, vmem),
        scratch_shapes=[pltpu.VMEM(w_out.shape, BF), pltpu.SemaphoreType.DMA],
        compiler_params=pltpu.CompilerParams(vmem_limit_bytes=16 * MIB),
        cost_estimate=pl.CostEstimate(
            flops=2 * hist * here * width * width, bytes_accessed=5 * 1024 * 1024, transcendentals=0
        ),
        name="finish",
    )(tag, listed, events, w_out, *keeps, *received)


def score_kernel(sources, tag_ref, base_ref, rows_ref, more_ref, label_ref, *refs):
    tables = refs[:sources]
    outs = refs[sources:-2]
    total, shares = refs[-2:]
    rows = rows_ref[...] + more_ref[...]
    label = label_ref[...]
    scale = D ** (-0.5)
    total[...] = jnp.zeros_like(total)
    which = 0
    for ref in tables:
        per = ref.shape[0]
        items = ref.shape[1] - PAD

        def one(i, which=which, ref=ref, items=items):
            table = ref[i, :items, :]
            bias = ref[i, items : items + 1, :items].astype(F32)
            logits = lax.dot_general(
                rows, table, (((1,), (1,)), ((), ())), preferred_element_type=F32
            )
            logits = logits * scale + bias
            ids = base_ref[which + i] + lax.broadcasted_iota(jnp.int32, (1, items), 1)
            target = (label == ids).astype(F32)
            coef = (1.0 / (1.0 + jnp.exp(-logits)) - target).astype(BF)
            total[...] += jnp.dot(coef, table, preferred_element_type=F32)

        if per <= 4:
            for i in range(per):
                one(i)
        else:
            pl.loop(0, per)(one)
        which += per
    count = len(outs)
    share, hist, _ = outs[0].shape
    for chip in range(count):
        for at in range(share):
            first = (chip * share + at) * hist
            shares[chip, at] = total[first : first + hist, :]
    for step, out in enumerate(outs):
        out[...] = shares[lax.rem(tag_ref[1] + step, count)].astype(out.dtype)


def score(tag, bases, rows, more, labels, tables, chips, hist):
    count, width = rows.shape
    share = count // chips // hist
    vmem = pl.BlockSpec(memory_space=pltpu.VMEM)
    smem = pl.BlockSpec(memory_space=pltpu.SMEM)
    own = jax.ShapeDtypeStruct((share, hist, width), F32)
    part = jax.ShapeDtypeStruct((share, hist, width), F32)
    return pl.pallas_call(
        functools.partial(score_kernel, len(tables)),
        out_shape=(own,) + (part,) * (chips - 1),
        in_specs=[smem, smem] + [vmem] * (3 + len(tables)),
        out_specs=(vmem,) * chips,
        scratch_shapes=[
            pltpu.VMEM((count, width), F32),
            pltpu.VMEM((chips, share, hist, width), F32),
        ],
        compiler_params=pltpu.CompilerParams(vmem_limit_bytes=8 * MIB + 3 * sum(t.size for t in tables)),
        cost_estimate=pl.CostEstimate(
            flops=4 * count * width * 1024, bytes_accessed=3 * 1024 * 1024, transcendentals=count * 1024
        ),
        name="score",
    )(tag, bases, rows, more, labels, *tables)


def on_device(events, w_in, w_out, item_table, item_bias, segment_lengths, listed_pos, labels):
    hist, here, width = events.shape
    seq = lax.axis_size("seq")
    batch = lax.axis_size("batch")
    chips = seq // 2
    rank = lax.axis_index("seq").astype(jnp.int32)
    mine = lax.axis_index("batch").astype(jnp.int32)
    place, core = rank // 2, rank % 2
    grid = batch == 4

    def swap(value):
        return lax.ppermute(value, "seq", [(i, i ^ 1) for i in range(seq)])

    def across(value, bit):
        return lax.ppermute(value, "batch", [(i, i ^ bit) for i in range(batch)])

    def ahead(value, by):
        return lax.ppermute(value, "seq", [(i, i + 2 * by) for i in range(seq - 2 * by)])

    half = width // 2
    chunks = []
    offset = core * half
    if grid:
        first = []
        for cols in CHUNKS:
            own = lax.dynamic_slice_in_dim(w_in, offset, cols, 1)
            offset = offset + cols
            if not chunks:
                over_x, over_y = across(own, 1), across(own, 2)
                first = [own, over_x, over_y]
                top = across(over_y[: width // 2], 1)
                bottom = across(over_x[width // 2 :], 2)
                chunks.append((first + [top, bottom], (0, 1, 2, 3, 3)))
            else:
                own, _ = lax.optimization_barrier((own, chunks[0][0]))
                chunks.append(([own] + [across(own, bit) for bit in (1, 2, 3)], (0, 1, 2, 3)))
        flip = mine
    else:
        whole = lax.all_gather(w_in, "batch", axis=1, tiled=True)
        for cols in CHUNKS:
            groups = [
                lax.dynamic_slice_in_dim(whole, group * width + offset, cols, 1)
                for group in range(4)
            ]
            chunks.append((groups, (0, 1, 2, 3)))
            offset = offset + cols
        flip = jnp.int32(0)

    longest = seq * here // 2
    reach = min(chips - 1, -(-(longest - 1) // (2 * here)))
    window = [events]
    for back in range(reach):
        last = window[-1]
        if grid and back == 0:
            last, _ = lax.optimization_barrier((last, first[0]))
        window.append(ahead(last, 1))
    blocks = []
    for back, block in enumerate(window):
        source = block
        if back == 0:
            source, _ = lax.optimization_barrier((block, window[1]))
        blocks += [block, swap(source)]

    tag = jnp.stack([flip, place, core])
    keeps, received = [], []
    for (weights, split), cols in zip(chunks, CHUNKS):
        keep, send = attend(tag, segment_lengths, blocks, weights, split, cols)
        keeps.append(keep)
        received.append(swap(send))

    share = listed_pos.shape[0] // seq
    local = listed_pos - rank * here
    inside = (local >= 0) & (local < here)
    index = jnp.where(inside, local + here * jnp.arange(hist, dtype=jnp.int32)[None, :], -1)

    def halves(value):
        value = value.reshape(chips, 2, share, hist).transpose(1, 0, 2, 3)
        return value.reshape(2, chips * share * hist, 1)

    index = halves(index)
    index = jnp.where(core == 0, index, index[::-1])
    own_labels = halves(labels)
    own_labels = jnp.where(core == 0, own_labels[0], own_labels[1])
    layer_out, rows, rows_send = finish(tag, index, events, w_out, keeps, received)
    rows = rows + swap(rows_send)
    step = 1
    near, more = rows, jnp.zeros_like(rows)
    while step < chips:
        if step > 1:
            rows = near = rows + more
        more = lax.ppermute(rows, "seq", [(i, i ^ (2 * step)) for i in range(seq)])
        step *= 2

    items = item_table.shape[0]
    item_table, _ = lax.optimization_barrier((item_table, window[-1]))
    padded = jnp.concatenate(
        [
            item_table,
            jnp.pad(item_bias[None, :], ((0, PAD - 1), (0, width - items))),
        ],
        0,
    )
    if grid:
        tables = [padded, across(padded, 1), across(padded, 2), across(padded, 3)]
        tables, _ = lax.optimization_barrier((tables, near))
        tables = [piece[None] for piece in tables]
        holder = mine ^ jnp.arange(4, dtype=jnp.int32)
    else:
        tables = [lax.all_gather(padded[None], "batch", axis=0, tiled=True)]
        holder = jnp.arange(batch, dtype=jnp.int32)
    tables = tables + [swap(piece) for piece in tables]
    bases = jnp.concatenate(
        [(rank * batch + holder) * items, ((rank ^ 1) * batch + holder) * items]
    )
    parts = score(tag, bases, rows, more, own_labels, tables, chips, hist)
    total = parts[0]
    for step in range(1, chips):
        arrived = lax.ppermute(
            parts[step], "seq", [(i, (i + 2 * step) % seq) for i in range(seq)]
        )
        total = total + arrived.astype(F32)
    return layer_out, total


def solution(mesh):
    return jax.shard_map(
        on_device,
        mesh=mesh,
        in_specs=(
            P("batch", "seq", None),
            P(None, "batch"),
            P(),
            P(("seq", "batch"), None),
            P(("seq", "batch")),
            P("batch", None),
            P(None, "batch"),
            P(None, "batch"),
        ),
        out_specs=(P("batch", "seq", None), P("seq", "batch", None)),
        check_vma=False,
    )
```

```python
import functools

import jax
import jax.numpy as jnp
from jax import lax
from jax.experimental import pallas as pl
from jax.experimental.pallas import tpu as pltpu
from jax.sharding import PartitionSpec as P

HEADS = 16
HD = 64
D = 1024
BF = jnp.bfloat16
F32 = jnp.float32
CHUNKS = (512,)
PAD = 16
MIB = 1024 * 1024


def silu_half(half):
    return half + half * jnp.tanh(half)


def attend_kernel(blocks, split, tag_ref, seg_ref, *refs):
    sources = refs[:blocks]
    pieces = refs[blocks : blocks + len(split)]
    keep_ref, send_ref, events, weights, acts, mask, accum, event_sem, weight_sem = refs[blocks + len(split) :]
    _, hist, here, width = events.shape
    cols = keep_ref.shape[-1]
    flip, place, core = tag_ref[0], tag_ref[1], tag_ref[2]
    chip = 2 * here

    bases, seen = [], {}
    for ref, slot in zip(pieces, split):
        bases.append(seen.get(slot, 0))
        seen[slot] = bases[-1] + ref.shape[0]

    def event_copy(block):
        return pltpu.make_async_copy(sources[block], events.at[block], event_sem.at[block])

    def weight_copy(at):
        rows = pl.ds(bases[at], pieces[at].shape[0])
        return pltpu.make_async_copy(pieces[at], weights.at[split[at], rows], weight_sem.at[at])

    event_copy(0).start()
    weight_copy(0).start()
    event_copy(1).start()
    for at in range(1, len(split)):
        weight_copy(at).start()
    for block in range(2, blocks):
        event_copy(block).start()

    def positions(shape, dim, back):
        at = lax.broadcasted_iota(jnp.int32, shape, dim)
        first = (at < here).astype(jnp.int32)
        rank = first * core + (1 - first) * (1 - core)
        return (place - back) * chip + rank * here + at - (1 - first) * here

    for h in range(hist):
        row = positions((chip, 1), 0, 0)
        start = jnp.zeros((chip, 1), jnp.int32)
        end = jnp.int32(0)
        for k in range(seg_ref.shape[1]):
            end = end + seg_ref[h, k]
            start = start + jnp.where(row >= end, seg_ref[h, k], 0)
        for back in range(blocks // 2):
            col = positions((1, chip), 1, back)
            allowed = (col <= row) & (col >= start)
            mask[h, back] = jnp.where(allowed, 1.0, 0.0).astype(F32)

    def project(slot, block):
        rows = events[block].reshape(hist * here, width)
        total = jnp.dot(rows, weights[slot], preferred_element_type=F32)
        acts[slot, block] = silu_half(0.5 * total).astype(BF).reshape(hist, here, cols)

    for slot in range(4):
        for at, owner in enumerate(split):
            if owner == slot:
                weight_copy(at).wait()
        for block in range(2):
            if slot == 0:
                event_copy(block).wait()
            project(slot, block)
    for block in range(2, blocks):
        event_copy(block).wait()
    for slot in range(4):

        @pl.when(((flip ^ slot) & 1) == 1)
        def _(slot=slot):
            for block in range(2, blocks):
                project(slot, block)

    gate, value, query, key = flip, flip ^ 1, flip ^ 2, flip ^ 3
    keep_ref[1] = acts[gate, 0]
    send_ref[1] = acts[gate, 1]
    lane = lax.broadcasted_iota(jnp.int32, (1, 128), 1)
    low = (lane < HD).astype(BF)
    high = 1 - low
    for h in range(hist):
        accum[...] = jnp.zeros_like(accum)
        first_row = place * chip
        first_start, end = jnp.int32(0), jnp.int32(0)
        for k in range(seg_ref.shape[1]):
            end = end + seg_ref[h, k]
            first_start = first_start + jnp.where(first_row >= end, seg_ref[h, k], 0)
        for back in range(blocks // 2):

            @pl.when(first_start < (place - back + 1) * chip)
            def _(h=h, back=back):
                allowed = mask[h, back]
                for pair in range(cols // 128):
                    at = slice(pair * 128, pair * 128 + 128)
                    q = jnp.concatenate([acts[query, 0, h, :, at], acts[query, 1, h, :, at]], 0)
                    k = jnp.concatenate(
                        [acts[key, 2 * back, h, :, at], acts[key, 2 * back + 1, h, :, at]], 0
                    )
                    v = jnp.concatenate(
                        [acts[value, 2 * back, h, :, at], acts[value, 2 * back + 1, h, :, at]], 0
                    )
                    q = q * jnp.asarray(0.5, BF)
                    total = accum[:, at]
                    for lanes in (low, high):
                        half = lax.dot_general(
                            q * lanes, k, (((1,), (1,)), ((), ())), preferred_element_type=F32
                        )
                        w = silu_half(half * allowed).astype(BF)
                        total = total + jnp.dot(w, v * lanes, preferred_element_type=F32)
                    accum[:, at] = total

        keep_ref[0, h] = accum[:here].astype(BF)
        send_ref[0, h] = accum[here:].astype(BF)


def attend(tag, lengths, events, weights, split, cols):
    hist, here, width = events[0].shape
    blocks = len(events)
    part = jax.ShapeDtypeStruct((2, hist, here, cols), BF)
    vmem = pl.BlockSpec(memory_space=pltpu.VMEM)
    smem = pl.BlockSpec(memory_space=pltpu.SMEM)
    flops = 2 * hist * here * width * cols * (2 * blocks + 4) + 8 * hist * 2 * here * here * blocks * cols
    return pl.pallas_call(
        functools.partial(attend_kernel, blocks, split),
        out_shape=(part, part),
        in_specs=[smem, smem] + [pl.BlockSpec(memory_space=pltpu.HBM)] * (blocks + len(weights)),
        out_specs=(vmem, vmem),
        scratch_shapes=[
            pltpu.VMEM((blocks, hist, here, width), BF),
            pltpu.VMEM((4, width, cols), BF),
            pltpu.VMEM((4, blocks, hist, here, cols), BF),
            pltpu.VMEM((hist, blocks // 2, 2 * here, 2 * here), F32),
            pltpu.VMEM((2 * here, cols), F32),
            pltpu.SemaphoreType.DMA((blocks,)),
            pltpu.SemaphoreType.DMA((len(split),)),
        ],
        compiler_params=pltpu.CompilerParams(vmem_limit_bytes=60 * MIB),
        cost_estimate=pl.CostEstimate(
            flops=flops, bytes_accessed=4 * 1024 * 1024, transcendentals=hist * here * 2 * here * blocks * cols // HD
        ),
        name="attend",
    )(tag, lengths, *events, *weights)


def column_of(ref, core, share, count):
    hist, listed = ref.shape
    row = lax.broadcasted_iota(jnp.int32, (count, 1), 0)
    lane = lax.broadcasted_iota(jnp.int32, (1, listed), 1)
    bits, more = hist.bit_length() - 1, share.bit_length() - 1
    which = row & (hist - 1)
    place = (row >> (bits + more)) * (2 * share) + core * share + ((row >> bits) & (share - 1))
    total = jnp.zeros((count, 1), F32)
    for h in range(hist):
        chosen = (lane == place) & (which == h)
        values = jnp.where(chosen, ref[h : h + 1, :].astype(F32), 0.0)
        total = total + jnp.sum(values, axis=1, keepdims=True)
    return total.astype(jnp.int32), which


def finish_kernel(count, share, tag_ref, listed_ref, events_ref, w_out_ref, *refs):
    parts = refs[: 2 * count]
    layer_ref, keep_ref, send_ref, matrix, matrix_sem = refs[2 * count :]
    copy = pltpu.make_async_copy(w_out_ref, matrix, matrix_sem)
    copy.start()
    hist, here, width = events_ref.shape
    rows = hist * here
    core = tag_ref[2]
    pieces, gates, offsets = [], [], []
    for side in range(2):
        base = (core ^ side) * (width // 2)
        for ref in parts[side * count : (side + 1) * count]:
            cols = ref.shape[-1]
            pieces.append(ref[0].reshape(rows, cols).astype(F32))
            gates.append(ref[1].reshape(rows, cols).astype(F32))
            offsets.append(pl.multiple_of(base, 128))
            base = base + cols
    mean = sum(jnp.sum(p, axis=1, keepdims=True) for p in pieces) * (1.0 / width)
    pieces = [p - mean for p in pieces]
    spread = sum(jnp.sum(p * p, axis=1, keepdims=True) for p in pieces) * (1.0 / width)
    inverse = lax.rsqrt(spread + 1e-05)
    output = events_ref[...].reshape(rows, width).astype(F32)
    copy.wait()
    for p, g, at in zip(pieces, gates, offsets):
        mixed = (p * inverse * g).astype(BF)
        output = output + jnp.dot(
            mixed, matrix[pl.ds(at, p.shape[1]), :], preferred_element_type=F32
        )
    layer = output.astype(BF)
    layer_ref[...] = layer.reshape(hist, here, width)
    column = lax.broadcasted_iota(jnp.int32, (1, rows), 1)
    for side, out_ref in ((0, keep_ref), (1, send_ref)):
        at, which = column_of(listed_ref, core ^ side, share, out_ref.shape[0])
        local = at - (2 * tag_ref[1] + core) * here
        inside = (local >= 0) & (local < here)
        pick = (jnp.where(inside, local + which * here, -1) == column).astype(BF)
        out_ref[...] = jnp.dot(pick, layer, preferred_element_type=F32).astype(BF)


def finish(tag, listed, events, w_out, keeps, received, share):
    hist, here, width = events.shape
    rows = listed.size // 2
    vmem = pl.BlockSpec(memory_space=pltpu.VMEM)
    smem = pl.BlockSpec(memory_space=pltpu.SMEM)
    return pl.pallas_call(
        functools.partial(finish_kernel, len(keeps), share),
        out_shape=(
            jax.ShapeDtypeStruct((hist, here, width), BF),
            jax.ShapeDtypeStruct((rows, width), BF),
            jax.ShapeDtypeStruct((rows, width), BF),
        ),
        in_specs=[smem, vmem, vmem, pl.BlockSpec(memory_space=pltpu.HBM)] + [vmem] * (len(keeps) + len(received)),
        out_specs=(vmem, vmem, vmem),
        scratch_shapes=[pltpu.VMEM(w_out.shape, BF), pltpu.SemaphoreType.DMA],
        compiler_params=pltpu.CompilerParams(vmem_limit_bytes=16 * MIB),
        cost_estimate=pl.CostEstimate(
            flops=2 * hist * here * width * width, bytes_accessed=5 * 1024 * 1024, transcendentals=0
        ),
        name="finish",
    )(tag, listed, events, w_out, *keeps, *received)


def score_kernel(sources, chip_size, batch, tag_ref, rows_ref, more_ref, label_ref, listed_ref, *refs):
    tables = refs[:sources]
    outs = refs[sources:-2]
    total, shares = refs[-2:]
    rows = rows_ref[...] + more_ref[...]
    share, hist, _ = outs[0].shape
    label, _ = column_of(label_ref, tag_ref[2], share, rows.shape[0])
    listed, _ = column_of(listed_ref, tag_ref[2], share, rows.shape[0])
    here = ((listed & chip_size) > 0) == ((tag_ref[1] & 1) > 0)
    scale = D ** (-0.5)
    total[...] = jnp.zeros_like(total)
    which = 0
    for number, ref in enumerate(tables):
        per = ref.shape[0]
        other = int(number >= sources // 2)
        if number == sources // 2:
            which = 0
        items = ref.shape[1] - PAD

        def one(i, which=which, ref=ref, items=items, other=other):
            owner = (2 * tag_ref[1] + tag_ref[2]) ^ (other + 2 * ((which + i) & 1))
            base = (owner * batch + (((which + i) >> 1) ^ tag_ref[0])) * items
            table = ref[i, :items, :]
            bias = ref[i, items : items + 1, :items].astype(F32)
            logits = lax.dot_general(
                rows, table, (((1,), (1,)), ((), ())), preferred_element_type=F32
            )
            logits = logits * scale + bias
            ids = base + lax.broadcasted_iota(jnp.int32, (1, items), 1)
            target = (label == ids).astype(F32)
            coef = 1.0 / (1.0 + jnp.exp(-logits)) - target
            coef = jnp.where(here, coef, 0.0).astype(BF)
            total[...] += jnp.dot(coef, table, preferred_element_type=F32)

        if per <= 4:
            for i in range(per):
                one(i)
        else:
            pl.loop(0, per)(one)
        which += per
    count = len(outs)
    for chip in range(count):
        for at in range(share):
            first = (chip * share + at) * hist
            shares[chip, at] = total[first : first + hist, :]
    for step, out in enumerate(outs):
        out[...] = shares[lax.rem(tag_ref[1] + step, count)].astype(out.dtype)


def score(tag, rows, more, labels, listed, tables, chips, hist, chip_size, batch):
    count, width = rows.shape
    share = count // chips // hist
    vmem = pl.BlockSpec(memory_space=pltpu.VMEM)
    smem = pl.BlockSpec(memory_space=pltpu.SMEM)
    own = jax.ShapeDtypeStruct((share, hist, width), F32)
    part = jax.ShapeDtypeStruct((share, hist, width), F32)
    return pl.pallas_call(
        functools.partial(score_kernel, len(tables), chip_size, batch),
        out_shape=(own,) + (part,) * (chips - 1),
        in_specs=[smem] + [vmem] * (4 + len(tables)),
        out_specs=(vmem,) * chips,
        scratch_shapes=[
            pltpu.VMEM((count, width), F32),
            pltpu.VMEM((chips, share, hist, width), F32),
        ],
        compiler_params=pltpu.CompilerParams(vmem_limit_bytes=8 * MIB + 3 * sum(t.size for t in tables)),
        cost_estimate=pl.CostEstimate(
            flops=4 * count * width * 1024, bytes_accessed=3 * 1024 * 1024, transcendentals=count * 1024
        ),
        name="score",
    )(tag, rows, more, labels, listed, *tables)


def on_device(events, w_in, w_out, item_table, item_bias, segment_lengths, listed_pos, labels):
    hist, here, width = events.shape
    seq = lax.axis_size("seq")
    batch = lax.axis_size("batch")
    chips = seq // 2
    rank = lax.axis_index("seq").astype(jnp.int32)
    mine = lax.axis_index("batch").astype(jnp.int32)
    place, core = rank // 2, rank % 2
    grid = batch == 4

    def swap(value):
        return lax.ppermute(value, "seq", [(i, i ^ 1) for i in range(seq)])

    def across(value, bit):
        return lax.ppermute(value, "batch", [(i, i ^ bit) for i in range(batch)])

    def ahead(value, by):
        return lax.ppermute(value, "seq", [(i, i + 2 * by) for i in range(seq - 2 * by)])

    half = width // 2
    chunks = []
    offset = core * half
    if grid:
        first = []
        for cols in CHUNKS:
            own = lax.dynamic_slice_in_dim(w_in, offset, cols, 1)
            offset = offset + cols
            if not chunks:
                over_x, over_y = across(own, 1), across(own, 2)
                first = [own, over_x, over_y]
                top = across(over_y[: width // 2], 1)
                bottom = across(over_x[width // 2 :], 2)
                chunks.append((first + [top, bottom], (0, 1, 2, 3, 3)))
            else:
                own, _ = lax.optimization_barrier((own, chunks[0][0]))
                chunks.append(([own] + [across(own, bit) for bit in (1, 2, 3)], (0, 1, 2, 3)))
        flip = mine
    else:
        whole = lax.all_gather(w_in, "batch", axis=1, tiled=True)
        for cols in CHUNKS:
            groups = [
                lax.dynamic_slice_in_dim(whole, group * width + offset, cols, 1)
                for group in range(4)
            ]
            chunks.append((groups, (0, 1, 2, 3)))
            offset = offset + cols
        flip = jnp.int32(0)

    longest = seq * here // 2
    reach = min(chips - 1, -(-(longest - 1) // (2 * here)))
    window = [events]
    for back in range(reach):
        last = window[-1]
        if grid and back == 0:
            last, _ = lax.optimization_barrier((last, first[0]))
        window.append(ahead(last, 1))
    blocks = []
    for back, block in enumerate(window):
        source = block
        if back == 0:
            source, _ = lax.optimization_barrier((block, window[1]))
        blocks += [block, swap(source)]

    tag = jnp.stack([flip, place, core])
    keeps, received = [], []
    for (weights, split), cols in zip(chunks, CHUNKS):
        keep, send = attend(tag, segment_lengths, blocks, weights, split, cols)
        keeps.append(keep)
        received.append(swap(send))

    share = listed_pos.shape[0] // seq
    listed, wanted = listed_pos.T, labels.T

    items = item_table.shape[0]
    padded = jnp.concatenate(
        [
            item_table,
            jnp.pad(item_bias[None, :], ((0, PAD - 1), (0, width - items))),
        ],
        0,
    )
    paired = lax.ppermute(padded, "seq", [(i, i ^ 2) for i in range(seq)])
    both = jnp.stack([padded, paired])
    if grid:
        both, _ = lax.optimization_barrier((both, (top, bottom)))
        tables = [both, across(both, 1), across(both, 2), across(both, 3)]
        ready, _ = lax.optimization_barrier((tag, tables[1:3]))
    else:
        tables = [lax.all_gather(both, "batch", axis=0, tiled=True)]
        ready = tag

    layer_out, rows, rows_send = finish(ready, listed, events, w_out, keeps, received, share)
    rows = rows + swap(rows_send)
    if grid:
        tables[:3], _ = lax.optimization_barrier((tables[:3], rows))
    more = jnp.zeros_like(rows)
    step = 2
    while step < chips:
        if step > 2:
            rows = rows + more
        more = lax.ppermute(rows, "seq", [(i, i ^ (2 * step)) for i in range(seq)])
        step *= 2
    if grid:
        tables[3], more = lax.optimization_barrier((tables[3], more))
    tables = tables + [swap(piece) for piece in tables]

    parts = score(tag, rows, more, wanted, listed, tables, chips, hist, 2 * here, batch)
    total = parts[0]
    for step in range(1, chips):
        arrived = lax.ppermute(
            parts[step], "seq", [(i, (i + 2 * step) % seq) for i in range(seq)]
        )
        total = total + arrived.astype(F32)
    return layer_out, total


def solution(mesh):
    return jax.shard_map(
        on_device,
        mesh=mesh,
        in_specs=(
            P("batch", "seq", None),
            P(None, "batch"),
            P(),
            P(("seq", "batch"), None),
            P(("seq", "batch")),
            P("batch", None),
            P(None, "batch"),
            P(None, "batch"),
        ),
        out_specs=(P("batch", "seq", None), P("seq", "batch", None)),
        check_vma=False,
    )
```

```python
import functools

import jax
import jax.numpy as jnp
from jax import lax
from jax.experimental import pallas as pl
from jax.experimental.pallas import tpu as pltpu
from jax.sharding import PartitionSpec as P

HEADS = 16
HD = 64
D = 1024
BF = jnp.bfloat16
F32 = jnp.float32
CHUNKS = (512,)
PAD = 16
MIB = 1024 * 1024


def silu_half(half):
    return half + half * jnp.tanh(half)


def attend_kernel(blocks, split, tag_ref, seg_ref, *refs):
    sources = refs[:blocks]
    pieces = refs[blocks : blocks + len(split)]
    keep_ref, send_ref, events, weights, acts, mask, accum, event_sem, weight_sem = refs[blocks + len(split) :]
    _, hist, here, width = events.shape
    cols = keep_ref.shape[-1]
    flip, place, core = tag_ref[0], tag_ref[1], tag_ref[2]
    chip = 2 * here

    bases, seen = [], {}
    for ref, slot in zip(pieces, split):
        bases.append(seen.get(slot, 0))
        seen[slot] = bases[-1] + ref.shape[0]

    def event_copy(block):
        return pltpu.make_async_copy(sources[block], events.at[block], event_sem.at[block])

    def weight_copy(at):
        rows = pl.ds(bases[at], pieces[at].shape[0])
        return pltpu.make_async_copy(pieces[at], weights.at[split[at], rows], weight_sem.at[at])

    event_copy(0).start()
    weight_copy(0).start()
    event_copy(1).start()
    for at in range(1, len(split)):
        weight_copy(at).start()
    for block in range(2, blocks):
        event_copy(block).start()

    def positions(shape, dim, back):
        at = lax.broadcasted_iota(jnp.int32, shape, dim)
        first = (at < here).astype(jnp.int32)
        rank = first * core + (1 - first) * (1 - core)
        return (place - back) * chip + rank * here + at - (1 - first) * here

    for h in range(hist):
        row = positions((chip, 1), 0, 0)
        start = jnp.zeros((chip, 1), jnp.int32)
        end = jnp.int32(0)
        for k in range(seg_ref.shape[1]):
            end = end + seg_ref[h, k]
            start = start + jnp.where(row >= end, seg_ref[h, k], 0)
        for back in range(blocks // 2):
            col = positions((1, chip), 1, back)
            allowed = (col <= row) & (col >= start)
            mask[h, back] = jnp.where(allowed, 1.0, 0.0).astype(F32)

    def project(slot, block):
        rows = events[block].reshape(hist * here, width)
        total = jnp.dot(rows, weights[slot], preferred_element_type=F32)
        acts[slot, block] = silu_half(0.5 * total).astype(BF).reshape(hist, here, cols)

    for slot in range(4):
        for at, owner in enumerate(split):
            if owner == slot:
                weight_copy(at).wait()
        for block in range(2):
            if slot == 0:
                event_copy(block).wait()
            project(slot, block)
    for block in range(2, blocks):
        event_copy(block).wait()
    for slot in range(4):

        @pl.when(((flip ^ slot) & 1) == 1)
        def _(slot=slot):
            for block in range(2, blocks):
                project(slot, block)

    gate, value, query, key = flip, flip ^ 1, flip ^ 2, flip ^ 3
    keep_ref[1] = acts[gate, 0]
    send_ref[1] = acts[gate, 1]
    lane = lax.broadcasted_iota(jnp.int32, (1, 128), 1)
    low = (lane < HD).astype(BF)
    high = 1 - low
    for h in range(hist):
        accum[...] = jnp.zeros_like(accum)
        first_row = place * chip
        first_start, end = jnp.int32(0), jnp.int32(0)
        for k in range(seg_ref.shape[1]):
            end = end + seg_ref[h, k]
            first_start = first_start + jnp.where(first_row >= end, seg_ref[h, k], 0)
        for back in range(blocks // 2):

            @pl.when(first_start < (place - back + 1) * chip)
            def _(h=h, back=back):
                allowed = mask[h, back]
                for pair in range(cols // 128):
                    at = slice(pair * 128, pair * 128 + 128)
                    q = jnp.concatenate([acts[query, 0, h, :, at], acts[query, 1, h, :, at]], 0)
                    k = jnp.concatenate(
                        [acts[key, 2 * back, h, :, at], acts[key, 2 * back + 1, h, :, at]], 0
                    )
                    v = jnp.concatenate(
                        [acts[value, 2 * back, h, :, at], acts[value, 2 * back + 1, h, :, at]], 0
                    )
                    q = q * jnp.asarray(0.5, BF)
                    total = accum[:, at]
                    for lanes in (low, high):
                        half = lax.dot_general(
                            q * lanes, k, (((1,), (1,)), ((), ())), preferred_element_type=F32
                        )
                        w = silu_half(half * allowed).astype(BF)
                        total = total + jnp.dot(w, v * lanes, preferred_element_type=F32)
                    accum[:, at] = total

        keep_ref[0, h] = accum[:here].astype(BF)
        send_ref[0, h] = accum[here:].astype(BF)


def attend(tag, lengths, events, weights, split, cols):
    hist, here, width = events[0].shape
    blocks = len(events)
    part = jax.ShapeDtypeStruct((2, hist, here, cols), BF)
    vmem = pl.BlockSpec(memory_space=pltpu.VMEM)
    smem = pl.BlockSpec(memory_space=pltpu.SMEM)
    flops = 2 * hist * here * width * cols * (2 * blocks + 4) + 8 * hist * 2 * here * here * blocks * cols
    return pl.pallas_call(
        functools.partial(attend_kernel, blocks, split),
        out_shape=(part, part),
        in_specs=[smem, smem] + [pl.BlockSpec(memory_space=pltpu.HBM)] * (blocks + len(weights)),
        out_specs=(vmem, vmem),
        scratch_shapes=[
            pltpu.VMEM((blocks, hist, here, width), BF),
            pltpu.VMEM((4, width, cols), BF),
            pltpu.VMEM((4, blocks, hist, here, cols), BF),
            pltpu.VMEM((hist, blocks // 2, 2 * here, 2 * here), F32),
            pltpu.VMEM((2 * here, cols), F32),
            pltpu.SemaphoreType.DMA((blocks,)),
            pltpu.SemaphoreType.DMA((len(split),)),
        ],
        compiler_params=pltpu.CompilerParams(vmem_limit_bytes=57 * MIB),
        cost_estimate=pl.CostEstimate(
            flops=flops, bytes_accessed=4 * 1024 * 1024, transcendentals=hist * here * 2 * here * blocks * cols // HD
        ),
        name="attend",
    )(tag, lengths, *events, *weights)


def column_of(ref, core, share, count):
    hist, listed = ref.shape
    row = lax.broadcasted_iota(jnp.int32, (count, 1), 0)
    lane = lax.broadcasted_iota(jnp.int32, (1, listed), 1)
    bits, more = hist.bit_length() - 1, share.bit_length() - 1
    which = row & (hist - 1)
    place = (row >> (bits + more)) * (2 * share) + core * share + ((row >> bits) & (share - 1))
    total = jnp.zeros((count, 1), F32)
    for h in range(hist):
        chosen = (lane == place) & (which == h)
        values = jnp.where(chosen, ref[h : h + 1, :].astype(F32), 0.0)
        total = total + jnp.sum(values, axis=1, keepdims=True)
    return total.astype(jnp.int32), which


def finish_kernel(count, share, tag_ref, listed_ref, events_ref, w_out_ref, *refs):
    parts = refs[: 2 * count]
    layer_ref, keep_ref, send_ref, matrix, matrix_sem = refs[2 * count :]
    copy = pltpu.make_async_copy(w_out_ref, matrix, matrix_sem)
    copy.start()
    hist, here, width = events_ref.shape
    rows = hist * here
    core = tag_ref[2]
    pieces, gates, offsets = [], [], []
    for side in range(2):
        base = (core ^ side) * (width // 2)
        for ref in parts[side * count : (side + 1) * count]:
            cols = ref.shape[-1]
            pieces.append(ref[0].reshape(rows, cols).astype(F32))
            gates.append(ref[1].reshape(rows, cols).astype(F32))
            offsets.append(pl.multiple_of(base, 128))
            base = base + cols
    mean = sum(jnp.sum(p, axis=1, keepdims=True) for p in pieces) * (1.0 / width)
    pieces = [p - mean for p in pieces]
    spread = sum(jnp.sum(p * p, axis=1, keepdims=True) for p in pieces) * (1.0 / width)
    inverse = lax.rsqrt(spread + 1e-05)
    output = events_ref[...].reshape(rows, width).astype(F32)
    copy.wait()
    for p, g, at in zip(pieces, gates, offsets):
        mixed = (p * inverse * g).astype(BF)
        output = output + jnp.dot(
            mixed, matrix[pl.ds(at, p.shape[1]), :], preferred_element_type=F32
        )
    layer = output.astype(BF)
    layer_ref[...] = layer.reshape(hist, here, width)
    column = lax.broadcasted_iota(jnp.int32, (1, rows), 1)
    for side, out_ref in ((0, keep_ref), (1, send_ref)):
        at, which = column_of(listed_ref, core ^ side, share, out_ref.shape[0])
        local = at - (2 * tag_ref[1] + core) * here
        inside = (local >= 0) & (local < here)
        pick = (jnp.where(inside, local + which * here, -1) == column).astype(BF)
        out_ref[...] = jnp.dot(pick, layer, preferred_element_type=F32).astype(BF)


def finish(tag, listed, events, w_out, keeps, received, share):
    hist, here, width = events.shape
    rows = listed.size // 2
    vmem = pl.BlockSpec(memory_space=pltpu.VMEM)
    smem = pl.BlockSpec(memory_space=pltpu.SMEM)
    return pl.pallas_call(
        functools.partial(finish_kernel, len(keeps), share),
        out_shape=(
            jax.ShapeDtypeStruct((hist, here, width), BF),
            jax.ShapeDtypeStruct((rows, width), BF),
            jax.ShapeDtypeStruct((rows, width), BF),
        ),
        in_specs=[smem, vmem, vmem, pl.BlockSpec(memory_space=pltpu.HBM)] + [vmem] * (len(keeps) + len(received)),
        out_specs=(vmem, vmem, vmem),
        scratch_shapes=[pltpu.VMEM(w_out.shape, BF), pltpu.SemaphoreType.DMA],
        compiler_params=pltpu.CompilerParams(vmem_limit_bytes=16 * MIB),
        cost_estimate=pl.CostEstimate(
            flops=2 * hist * here * width * width, bytes_accessed=5 * 1024 * 1024, transcendentals=0
        ),
        name="finish",
    )(tag, listed, events, w_out, *keeps, *received)


def score_kernel(sources, chip_size, batch, tag_ref, rows_ref, more_ref, label_ref, listed_ref, *refs):
    tables = refs[:sources]
    outs = refs[sources:-2]
    total, shares = refs[-2:]
    rows = rows_ref[...] + more_ref[...]
    share, hist, _ = outs[0].shape
    label, _ = column_of(label_ref, tag_ref[2], share, rows.shape[0])
    listed, _ = column_of(listed_ref, tag_ref[2], share, rows.shape[0])
    here = ((listed & chip_size) > 0) == ((tag_ref[1] & 1) > 0)
    scale = D ** (-0.5)
    total[...] = jnp.zeros_like(total)
    which = 0
    for number, ref in enumerate(tables):
        per = ref.shape[0]
        other = int(number >= sources // 2)
        if number == sources // 2:
            which = 0
        items = ref.shape[1] - PAD

        def one(i, which=which, ref=ref, items=items, other=other):
            owner = (2 * tag_ref[1] + tag_ref[2]) ^ (other + 2 * ((which + i) & 1))
            base = (owner * batch + (((which + i) >> 1) ^ tag_ref[0])) * items
            table = ref[i, :items, :]
            bias = ref[i, items : items + 1, :items].astype(F32)
            logits = lax.dot_general(
                rows, table, (((1,), (1,)), ((), ())), preferred_element_type=F32
            )
            logits = logits * scale + bias
            ids = base + lax.broadcasted_iota(jnp.int32, (1, items), 1)
            target = (label == ids).astype(F32)
            coef = 1.0 / (1.0 + jnp.exp(-logits)) - target
            coef = jnp.where(here, coef, 0.0).astype(BF)
            total[...] += jnp.dot(coef, table, preferred_element_type=F32)

        if per <= 4:
            for i in range(per):
                one(i)
        else:
            pl.loop(0, per)(one)
        which += per
    count = len(outs)
    for chip in range(count):
        for at in range(share):
            first = (chip * share + at) * hist
            shares[chip, at] = total[first : first + hist, :]
    for step, out in enumerate(outs):
        out[...] = shares[lax.rem(tag_ref[1] + step, count)].astype(out.dtype)


def score(tag, rows, more, labels, listed, tables, chips, hist, chip_size, batch):
    count, width = rows.shape
    share = count // chips // hist
    vmem = pl.BlockSpec(memory_space=pltpu.VMEM)
    smem = pl.BlockSpec(memory_space=pltpu.SMEM)
    own = jax.ShapeDtypeStruct((share, hist, width), F32)
    part = jax.ShapeDtypeStruct((share, hist, width), F32)
    return pl.pallas_call(
        functools.partial(score_kernel, len(tables), chip_size, batch),
        out_shape=(own,) + (part,) * (chips - 1),
        in_specs=[smem] + [vmem] * (4 + len(tables)),
        out_specs=(vmem,) * chips,
        scratch_shapes=[
            pltpu.VMEM((count, width), F32),
            pltpu.VMEM((chips, share, hist, width), F32),
        ],
        compiler_params=pltpu.CompilerParams(vmem_limit_bytes=8 * MIB + 3 * sum(t.size for t in tables)),
        cost_estimate=pl.CostEstimate(
            flops=4 * count * width * 1024, bytes_accessed=3 * 1024 * 1024, transcendentals=count * 1024
        ),
        name="score",
    )(tag, rows, more, labels, listed, *tables)


def on_device(events, w_in, w_out, item_table, item_bias, segment_lengths, listed_pos, labels):
    hist, here, width = events.shape
    seq = lax.axis_size("seq")
    batch = lax.axis_size("batch")
    chips = seq // 2
    rank = lax.axis_index("seq").astype(jnp.int32)
    mine = lax.axis_index("batch").astype(jnp.int32)
    place, core = rank // 2, rank % 2
    grid = batch == 4

    def swap(value):
        return lax.ppermute(value, "seq", [(i, i ^ 1) for i in range(seq)])

    def across(value, bit):
        return lax.ppermute(value, "batch", [(i, i ^ bit) for i in range(batch)])

    def ahead(value, by):
        return lax.ppermute(value, "seq", [(i, i + 2 * by) for i in range(seq - 2 * by)])

    half = width // 2
    chunks = []
    offset = core * half
    if grid:
        first = []
        for cols in CHUNKS:
            own = lax.dynamic_slice_in_dim(w_in, offset, cols, 1)
            offset = offset + cols
            if not chunks:
                over_x, over_y = across(own, 1), across(own, 2)
                first = [own, over_x, over_y]
                top = across(over_y[: width // 2], 1)
                bottom = across(over_x[width // 2 :], 2)
                chunks.append((first + [top, bottom], (0, 1, 2, 3, 3)))
            else:
                own, _ = lax.optimization_barrier((own, chunks[0][0]))
                chunks.append(([own] + [across(own, bit) for bit in (1, 2, 3)], (0, 1, 2, 3)))
        flip = mine
    else:
        whole = lax.all_gather(w_in, "batch", axis=1, tiled=True)
        for cols in CHUNKS:
            groups = [
                lax.dynamic_slice_in_dim(whole, group * width + offset, cols, 1)
                for group in range(4)
            ]
            chunks.append((groups, (0, 1, 2, 3)))
            offset = offset + cols
        flip = jnp.int32(0)

    longest = seq * here // 2
    reach = min(chips - 1, -(-(longest - 1) // (2 * here)))
    window = [events]
    for back in range(reach):
        last = window[-1]
        if grid and back == 0:
            last, _ = lax.optimization_barrier((last, first[0]))
        window.append(ahead(last, 1))
    blocks = []
    for back, block in enumerate(window):
        source = block
        if back == 0:
            source, _ = lax.optimization_barrier((block, window[1]))
        blocks += [block, swap(source)]

    tag = jnp.stack([flip, place, core])
    keeps, received = [], []
    for (weights, split), cols in zip(chunks, CHUNKS):
        keep, send = attend(tag, segment_lengths, blocks, weights, split, cols)
        keeps.append(keep)
        received.append(swap(send))

    share = listed_pos.shape[0] // seq
    listed, wanted = listed_pos.T, labels.T

    items = item_table.shape[0]
    padded = jnp.concatenate(
        [
            item_table,
            jnp.pad(item_bias[None, :], ((0, PAD - 1), (0, width - items))),
        ],
        0,
    )
    paired = lax.ppermute(padded, "seq", [(i, i ^ 2) for i in range(seq)])
    both = jnp.stack([padded, paired])
    if grid:
        both, _ = lax.optimization_barrier((both, (top, bottom)))
        tables = [both, across(both, 1), across(both, 2), across(both, 3)]
        ready, _ = lax.optimization_barrier((tag, tables[1:3]))
    else:
        tables = [lax.all_gather(both, "batch", axis=0, tiled=True)]
        ready = tag

    layer_out, rows, rows_send = finish(ready, listed, events, w_out, keeps, received, share)
    rows = rows + swap(rows_send)
    if grid:
        tables[:3], _ = lax.optimization_barrier((tables[:3], rows))
    more = jnp.zeros_like(rows)
    step = 2
    while step < chips:
        if step > 2:
            rows = rows + more
        more = lax.ppermute(rows, "seq", [(i, i ^ (2 * step)) for i in range(seq)])
        step *= 2
    if grid:
        tables[3], more = lax.optimization_barrier((tables[3], more))
    tables = tables + [swap(piece) for piece in tables]

    parts = score(tag, rows, more, wanted, listed, tables, chips, hist, 2 * here, batch)
    total = parts[0]
    for step in range(1, chips):
        arrived = lax.ppermute(
            parts[step], "seq", [(i, (i + 2 * step) % seq) for i in range(seq)]
        )
        total = total + arrived.astype(F32)
    return layer_out, total


def solution(mesh):
    return jax.shard_map(
        on_device,
        mesh=mesh,
        in_specs=(
            P("batch", "seq", None),
            P(None, "batch"),
            P(),
            P(("seq", "batch"), None),
            P(("seq", "batch")),
            P("batch", None),
            P(None, "batch"),
            P(None, "batch"),
        ),
        out_specs=(P("batch", "seq", None), P("seq", "batch", None)),
        check_vma=False,
    )
```

```python
import functools

import jax
import jax.numpy as jnp
from jax import lax
from jax.experimental import pallas as pl
from jax.experimental.pallas import tpu as pltpu
from jax.sharding import PartitionSpec as P

HEADS = 16
HD = 64
D = 1024
BF = jnp.bfloat16
F32 = jnp.float32
CHUNKS = (512,)
PAD = 16
MIB = 1024 * 1024


def silu_half(half):
    return half + half * jnp.tanh(half)


def attend_kernel(blocks, split, tag_ref, seg_ref, *refs):
    sources = refs[:blocks]
    pieces = refs[blocks : blocks + len(split)]
    keep_ref, send_ref, events, weights, acts, mask, accum, event_sem, weight_sem = refs[blocks + len(split) :]
    _, hist, here, width = events.shape
    cols = keep_ref.shape[-1]
    flip, place, core = tag_ref[0], tag_ref[1], tag_ref[2]
    chip = 2 * here

    bases, seen = [], {}
    for ref, slot in zip(pieces, split):
        bases.append(seen.get(slot, 0))
        seen[slot] = bases[-1] + ref.shape[0]

    def event_copy(block):
        return pltpu.make_async_copy(sources[block], events.at[block], event_sem.at[block])

    def weight_copy(at):
        rows = pl.ds(bases[at], pieces[at].shape[0])
        return pltpu.make_async_copy(pieces[at], weights.at[split[at], rows], weight_sem.at[at])

    event_copy(0).start()
    weight_copy(0).start()
    event_copy(1).start()
    for at in range(1, len(split)):
        weight_copy(at).start()
    for block in range(2, blocks):
        event_copy(block).start()

    def positions(shape, dim, back):
        at = lax.broadcasted_iota(jnp.int32, shape, dim)
        first = (at < here).astype(jnp.int32)
        rank = first * core + (1 - first) * (1 - core)
        return (place - back) * chip + rank * here + at - (1 - first) * here

    for h in range(hist):
        row = positions((chip, 1), 0, 0)
        start = jnp.zeros((chip, 1), jnp.int32)
        end = jnp.int32(0)
        for k in range(seg_ref.shape[1]):
            end = end + seg_ref[h, k]
            start = start + jnp.where(row >= end, seg_ref[h, k], 0)
        for back in range(blocks // 2):
            col = positions((1, chip), 1, back)
            allowed = (col <= row) & (col >= start)
            mask[h, back] = jnp.where(allowed, 1.0, 0.0).astype(F32)

    def project(slot, block):
        rows = events[block].reshape(hist * here, width)
        total = jnp.dot(rows, weights[slot], preferred_element_type=F32)
        acts[slot, block] = silu_half(0.5 * total).astype(BF).reshape(hist, here, cols)

    for slot in range(4):
        for at, owner in enumerate(split):
            if owner == slot:
                weight_copy(at).wait()
        for block in range(2):
            if slot == 0:
                event_copy(block).wait()
            project(slot, block)
    for block in range(2, blocks):
        event_copy(block).wait()
    for slot in range(4):

        @pl.when(((flip ^ slot) & 1) == 1)
        def _(slot=slot):
            for block in range(2, blocks):
                project(slot, block)

    gate, value, query, key = flip, flip ^ 1, flip ^ 2, flip ^ 3
    keep_ref[1] = acts[gate, 0]
    send_ref[1] = acts[gate, 1]
    lane = lax.broadcasted_iota(jnp.int32, (1, 128), 1)
    low = (lane < HD).astype(BF)
    high = 1 - low
    for h in range(hist):
        accum[...] = jnp.zeros_like(accum)
        first_row = place * chip
        first_start, end = jnp.int32(0), jnp.int32(0)
        for k in range(seg_ref.shape[1]):
            end = end + seg_ref[h, k]
            first_start = first_start + jnp.where(first_row >= end, seg_ref[h, k], 0)
        for back in range(blocks // 2):

            @pl.when(first_start < (place - back + 1) * chip)
            def _(h=h, back=back):
                allowed = mask[h, back]
                for pair in range(cols // 128):
                    at = slice(pair * 128, pair * 128 + 128)
                    q = jnp.concatenate([acts[query, 0, h, :, at], acts[query, 1, h, :, at]], 0)
                    k = jnp.concatenate(
                        [acts[key, 2 * back, h, :, at], acts[key, 2 * back + 1, h, :, at]], 0
                    )
                    v = jnp.concatenate(
                        [acts[value, 2 * back, h, :, at], acts[value, 2 * back + 1, h, :, at]], 0
                    )
                    q = q * jnp.asarray(0.5, BF)
                    total = accum[:, at]
                    for lanes in (low, high):
                        half = lax.dot_general(
                            q * lanes, k, (((1,), (1,)), ((), ())), preferred_element_type=F32
                        )
                        w = silu_half(half * allowed).astype(BF)
                        total = total + jnp.dot(w, v * lanes, preferred_element_type=F32)
                    accum[:, at] = total

        keep_ref[0, h] = accum[:here].astype(BF)
        send_ref[0, h] = accum[here:].astype(BF)


def attend(tag, lengths, events, weights, split, cols):
    hist, here, width = events[0].shape
    blocks = len(events)
    part = jax.ShapeDtypeStruct((2, hist, here, cols), BF)
    vmem = pl.BlockSpec(memory_space=pltpu.VMEM)
    smem = pl.BlockSpec(memory_space=pltpu.SMEM)
    flops = 2 * hist * here * width * cols * (2 * blocks + 4) + 8 * hist * 2 * here * here * blocks * cols
    return pl.pallas_call(
        functools.partial(attend_kernel, blocks, split),
        out_shape=(part, part),
        in_specs=[smem, smem] + [pl.BlockSpec(memory_space=pltpu.HBM)] * (blocks + len(weights)),
        out_specs=(vmem, vmem),
        scratch_shapes=[
            pltpu.VMEM((blocks, hist, here, width), BF),
            pltpu.VMEM((4, width, cols), BF),
            pltpu.VMEM((4, blocks, hist, here, cols), BF),
            pltpu.VMEM((hist, blocks // 2, 2 * here, 2 * here), F32),
            pltpu.VMEM((2 * here, cols), F32),
            pltpu.SemaphoreType.DMA((blocks,)),
            pltpu.SemaphoreType.DMA((len(split),)),
        ],
        compiler_params=pltpu.CompilerParams(vmem_limit_bytes=57 * MIB),
        cost_estimate=pl.CostEstimate(
            flops=flops, bytes_accessed=4 * 1024 * 1024, transcendentals=hist * here * 2 * here * blocks * cols // HD
        ),
        name="attend",
    )(tag, lengths, *events, *weights)


def column_of(ref, core, share, count):
    hist, listed = ref.shape
    row = lax.broadcasted_iota(jnp.int32, (count, 1), 0)
    lane = lax.broadcasted_iota(jnp.int32, (1, listed), 1)
    bits, more = hist.bit_length() - 1, share.bit_length() - 1
    which = row & (hist - 1)
    place = (row >> (bits + more)) * (2 * share) + core * share + ((row >> bits) & (share - 1))
    total = jnp.zeros((count, 1), F32)
    for h in range(hist):
        chosen = (lane == place) & (which == h)
        values = jnp.where(chosen, ref[h : h + 1, :].astype(F32), 0.0)
        total = total + jnp.sum(values, axis=1, keepdims=True)
    return total.astype(jnp.int32), which


def finish_kernel(count, share, tag_ref, listed_ref, events_ref, w_out_ref, *refs):
    parts = refs[: 2 * count]
    layer_ref, keep_ref, send_ref, matrix, matrix_sem = refs[2 * count :]
    copy = pltpu.make_async_copy(w_out_ref, matrix, matrix_sem)
    copy.start()
    hist, here, width = events_ref.shape
    rows = hist * here
    core = tag_ref[2]
    pieces, gates, offsets = [], [], []
    for side in range(2):
        base = (core ^ side) * (width // 2)
        for ref in parts[side * count : (side + 1) * count]:
            cols = ref.shape[-1]
            pieces.append(ref[0].reshape(rows, cols).astype(F32))
            gates.append(ref[1].reshape(rows, cols).astype(F32))
            offsets.append(pl.multiple_of(base, 128))
            base = base + cols
    mean = sum(jnp.sum(p, axis=1, keepdims=True) for p in pieces) * (1.0 / width)
    pieces = [p - mean for p in pieces]
    spread = sum(jnp.sum(p * p, axis=1, keepdims=True) for p in pieces) * (1.0 / width)
    inverse = lax.rsqrt(spread + 1e-05)
    output = events_ref[...].reshape(rows, width).astype(F32)
    copy.wait()
    for p, g, at in zip(pieces, gates, offsets):
        mixed = (p * inverse * g).astype(BF)
        output = output + jnp.dot(
            mixed, matrix[pl.ds(at, p.shape[1]), :], preferred_element_type=F32
        )
    layer = output.astype(BF)
    layer_ref[...] = layer.reshape(hist, here, width)
    column = lax.broadcasted_iota(jnp.int32, (1, rows), 1)
    for side, out_ref in ((0, keep_ref), (1, send_ref)):
        at, which = column_of(listed_ref, core ^ side, share, out_ref.shape[0])
        local = at - (2 * tag_ref[1] + core) * here
        inside = (local >= 0) & (local < here)
        pick = (jnp.where(inside, local + which * here, -1) == column).astype(BF)
        out_ref[...] = jnp.dot(pick, layer, preferred_element_type=F32).astype(BF)


def finish(tag, listed, events, w_out, keeps, received, share):
    hist, here, width = events.shape
    rows = listed.size // 2
    vmem = pl.BlockSpec(memory_space=pltpu.VMEM)
    smem = pl.BlockSpec(memory_space=pltpu.SMEM)
    return pl.pallas_call(
        functools.partial(finish_kernel, len(keeps), share),
        out_shape=(
            jax.ShapeDtypeStruct((hist, here, width), BF),
            jax.ShapeDtypeStruct((rows, width), BF),
            jax.ShapeDtypeStruct((rows, width), BF),
        ),
        in_specs=[smem, vmem, vmem, pl.BlockSpec(memory_space=pltpu.HBM)] + [vmem] * (len(keeps) + len(received)),
        out_specs=(vmem, vmem, vmem),
        scratch_shapes=[pltpu.VMEM(w_out.shape, BF), pltpu.SemaphoreType.DMA],
        compiler_params=pltpu.CompilerParams(vmem_limit_bytes=16 * MIB),
        cost_estimate=pl.CostEstimate(
            flops=2 * hist * here * width * width, bytes_accessed=5 * 1024 * 1024, transcendentals=0
        ),
        name="finish",
    )(tag, listed, events, w_out, *keeps, *received)


def score_kernel(sources, chip_size, batch, tag_ref, rows_ref, more_ref, label_ref, listed_ref, *refs):
    tables = refs[:sources]
    outs = refs[sources:-2]
    total, shares = refs[-2:]
    rows = rows_ref[...] + more_ref[...]
    share, hist, _ = outs[0].shape
    label, _ = column_of(label_ref, tag_ref[2], share, rows.shape[0])
    listed, _ = column_of(listed_ref, tag_ref[2], share, rows.shape[0])
    here = ((listed & chip_size) > 0) == ((tag_ref[1] & 1) > 0)
    scale = D ** (-0.5)
    total[...] = jnp.zeros_like(total)
    which = 0
    for number, ref in enumerate(tables):
        per = ref.shape[0]
        other = int(number >= sources // 2)
        if number == sources // 2:
            which = 0
        items = ref.shape[1] - PAD

        def one(i, which=which, ref=ref, items=items, other=other):
            owner = (2 * tag_ref[1] + tag_ref[2]) ^ (other + 2 * ((which + i) & 1))
            base = (owner * batch + (((which + i) >> 1) ^ tag_ref[0])) * items
            table = ref[i, :items, :]
            bias = ref[i, items : items + 1, :items].astype(F32)
            logits = lax.dot_general(
                rows, table, (((1,), (1,)), ((), ())), preferred_element_type=F32
            )
            logits = logits * scale + bias
            ids = base + lax.broadcasted_iota(jnp.int32, (1, items), 1)
            target = (label == ids).astype(F32)
            coef = 1.0 / (1.0 + jnp.exp(-logits)) - target
            coef = jnp.where(here, coef, 0.0).astype(BF)
            total[...] += jnp.dot(coef, table, preferred_element_type=F32)

        if per <= 4:
            for i in range(per):
                one(i)
        else:
            pl.loop(0, per)(one)
        which += per
    count = len(outs)
    for chip in range(count):
        for at in range(share):
            first = (chip * share + at) * hist
            shares[chip, at] = total[first : first + hist, :]
    for step, out in enumerate(outs):
        out[...] = shares[lax.rem(tag_ref[1] + step, count)].astype(out.dtype)


def score(tag, rows, more, labels, listed, tables, chips, hist, chip_size, batch):
    count, width = rows.shape
    share = count // chips // hist
    vmem = pl.BlockSpec(memory_space=pltpu.VMEM)
    smem = pl.BlockSpec(memory_space=pltpu.SMEM)
    own = jax.ShapeDtypeStruct((share, hist, width), F32)
    part = jax.ShapeDtypeStruct((share, hist, width), F32)
    return pl.pallas_call(
        functools.partial(score_kernel, len(tables), chip_size, batch),
        out_shape=(own,) + (part,) * (chips - 1),
        in_specs=[smem] + [vmem] * (4 + len(tables)),
        out_specs=(vmem,) * chips,
        scratch_shapes=[
            pltpu.VMEM((count, width), F32),
            pltpu.VMEM((chips, share, hist, width), F32),
        ],
        compiler_params=pltpu.CompilerParams(vmem_limit_bytes=8 * MIB + 3 * sum(t.size for t in tables)),
        cost_estimate=pl.CostEstimate(
            flops=4 * count * width * 1024, bytes_accessed=3 * 1024 * 1024, transcendentals=count * 1024
        ),
        name="score",
    )(tag, rows, more, labels, listed, *tables)


def on_device(events, w_in, w_out, item_table, item_bias, segment_lengths, listed_pos, labels):
    hist, here, width = events.shape
    seq = lax.axis_size("seq")
    batch = lax.axis_size("batch")
    chips = seq // 2
    rank = lax.axis_index("seq").astype(jnp.int32)
    mine = lax.axis_index("batch").astype(jnp.int32)
    place, core = rank // 2, rank % 2
    grid = batch == 4

    def swap(value):
        return lax.ppermute(value, "seq", [(i, i ^ 1) for i in range(seq)])

    def across(value, bit):
        return lax.ppermute(value, "batch", [(i, i ^ bit) for i in range(batch)])

    def ahead(value, by):
        return lax.ppermute(value, "seq", [(i, i + 2 * by) for i in range(seq - 2 * by)])

    half = width // 2
    chunks = []
    offset = core * half
    if grid:
        first = []
        for cols in CHUNKS:
            own = lax.dynamic_slice_in_dim(w_in, offset, cols, 1)
            offset = offset + cols
            if not chunks:
                upper, lower = own[: width // 2], own[width // 2 :]
                over_y = [across(upper, 2), across(lower, 2)]
                over_x = [across(upper, 1), across(lower, 1)]
                first = [own]
                top = across(over_y[0], 1)
                bottom = across(over_x[1], 2)
                chunks.append((first + over_x + over_y + [top, bottom], (0, 1, 1, 2, 2, 3, 3)))
            else:
                own, _ = lax.optimization_barrier((own, chunks[0][0]))
                chunks.append(([own] + [across(own, bit) for bit in (1, 2, 3)], (0, 1, 2, 3)))
        flip = mine
    else:
        whole = lax.all_gather(w_in, "batch", axis=1, tiled=True)
        for cols in CHUNKS:
            groups = [
                lax.dynamic_slice_in_dim(whole, group * width + offset, cols, 1)
                for group in range(4)
            ]
            chunks.append((groups, (0, 1, 2, 3)))
            offset = offset + cols
        flip = jnp.int32(0)

    longest = seq * here // 2
    reach = min(chips - 1, -(-(longest - 1) // (2 * here)))
    window = [events]
    for back in range(reach):
        last = window[-1]
        if grid and back == 0:
            last, _ = lax.optimization_barrier((last, first[0]))
        window.append(ahead(last, 1))
    blocks = []
    for back, block in enumerate(window):
        source = block
        if back == 0:
            source, _ = lax.optimization_barrier((block, window[1]))
        blocks += [block, swap(source)]

    tag = jnp.stack([flip, place, core])
    keeps, received = [], []
    for (weights, split), cols in zip(chunks, CHUNKS):
        keep, send = attend(tag, segment_lengths, blocks, weights, split, cols)
        keeps.append(keep)
        received.append(swap(send))

    share = listed_pos.shape[0] // seq
    listed, wanted = listed_pos.T, labels.T

    items = item_table.shape[0]
    padded = jnp.concatenate(
        [
            item_table,
            jnp.pad(item_bias[None, :], ((0, PAD - 1), (0, width - items))),
        ],
        0,
    )
    paired = lax.ppermute(padded, "seq", [(i, i ^ 2) for i in range(seq)])
    both = jnp.stack([padded, paired])
    if grid:
        both, _ = lax.optimization_barrier((both, (top, bottom)))
        tables = [both, across(both, 1), across(both, 2), across(both, 3)]
        ready, _ = lax.optimization_barrier((tag, tables[1:3]))
    else:
        tables = [lax.all_gather(both, "batch", axis=0, tiled=True)]
        ready = tag

    layer_out, rows, rows_send = finish(ready, listed, events, w_out, keeps, received, share)
    rows = rows + swap(rows_send)
    if grid:
        tables[:3], _ = lax.optimization_barrier((tables[:3], rows))
    more = jnp.zeros_like(rows)
    step = 2
    while step < chips:
        if step > 2:
            rows = rows + more
        more = lax.ppermute(rows, "seq", [(i, i ^ (2 * step)) for i in range(seq)])
        step *= 2
    if grid:
        tables[3], more = lax.optimization_barrier((tables[3], more))
    tables = tables + [swap(piece) for piece in tables]

    parts = score(tag, rows, more, wanted, listed, tables, chips, hist, 2 * here, batch)
    total = parts[0]
    for step in range(1, chips):
        arrived = lax.ppermute(
            parts[step], "seq", [(i, (i + 2 * step) % seq) for i in range(seq)]
        )
        total = total + arrived.astype(F32)
    return layer_out, total


def solution(mesh):
    return jax.shard_map(
        on_device,
        mesh=mesh,
        in_specs=(
            P("batch", "seq", None),
            P(None, "batch"),
            P(),
            P(("seq", "batch"), None),
            P(("seq", "batch")),
            P("batch", None),
            P(None, "batch"),
            P(None, "batch"),
        ),
        out_specs=(P("batch", "seq", None), P("seq", "batch", None)),
        check_vma=False,
    )
```
